256 devices in a mesh: row: 8 (over x_lo, y), col: 32 (over z, x_hi, core).
Axes of the slice: x: 4 (x_hi: 2, x_lo: 2; x = x_hi * 2 + x_lo), y: 4, z: 8, core: 2. Of those that a mesh axis runs over, the one named last changes fastest.
Arguments:
- a_values: bfloat16 [32, 128, 4096], P('col', 'row'), may hold values from -0.09375 to 0.09375
- a_rows: int32 [32, 128], P('col', 'row'), may hold values from 0 to 3, as said below
- a_cols: int32 [32, 128], P('col', 'row'), may hold values from 0 to 15, as said below
- a_count: int32 [32, 8], P('col', 'row'), may hold values from 4 to 16, as said below
- p_values: bfloat16 [8, 128, 4096], P('row', 'col'), may hold values from -1.5 to 1.5
- p_rows: int32 [8, 128], P('row', 'col'), may hold values from 0 to 15, as said below
- p_cols: int32 [8, 128], P('row', 'col'), may hold values from 0 to 1, as said below
- p_count: int32 [8, 32], P('row', 'col'), may hold values from 2 to 4, as said below
Outputs:
- coarse: float32 [4096, 4096], P('col', 'row')
The draws below stay inside these ranges and needn't reach their ends.
Inputs may be any that keep to these rules, and one draw needn't show every extreme that they name: `a_rows`: block rows within a panel of 4. `a_cols`: block columns within a panel of 16; no (row, column) pair appears twice in one device's list, unused slots included. `a_count`: slots at or past the count are ignored; some device is full. `p_rows`: block rows within a panel of 16. `p_cols`: block columns within a panel of 2; no (row, column) pair appears twice in one device's list, unused slots included. `p_count`: slots at or past the count are ignored; some device is full.
All inputs are finite; a program needn't handle non-finite values.
Results may differ from the reference program's by a relative error of at most 0.01.
Values may be sent and summed in bfloat16 or wider, within the bound.
A program may use at most 128 MiB of HBM per device.

```python
import jax
import jax.numpy as jnp
from jax import lax

BS = 64
FB_DEV = 4
CB_DEV = 2
RATIO = 4
NBF = 128
NBC = 64
NC = 4096
CAP_A = 16
CAP_P = 4
N_ROW = 8
N_COL = 32


def slot_table(key, slot_total, keep_count, devices):
    device_keys = jax.random.split(key, devices)
    return jax.vmap(lambda single: jax.random.permutation(single, slot_total)[:keep_count])(device_keys)


def draw_a_rows(key, part):
    chosen = slot_table(jax.random.fold_in(key, 4), FB_DEV * FB_DEV * RATIO, CAP_A, N_COL * N_ROW)
    return (chosen // (FB_DEV * RATIO)).reshape(N_COL, N_ROW * CAP_A).astype(jnp.int32)


def draw_a_cols(key, part):
    chosen = slot_table(jax.random.fold_in(key, 4), FB_DEV * FB_DEV * RATIO, CAP_A, N_COL * N_ROW)
    return (chosen % (FB_DEV * RATIO)).reshape(N_COL, N_ROW * CAP_A).astype(jnp.int32)


def draw_a_count(key, part):
    key = jax.random.fold_in(key, 11)
    lower = jax.random.randint(key, (N_COL, N_ROW), max(1, CAP_A // 4), max(2, CAP_A // 2) + 1)
    banded = jnp.arange(N_COL)[:, None] // RATIO == jnp.arange(N_ROW)[None, :]
    return jnp.where(banded, CAP_A, lower).astype(jnp.int32)


def draw_p_rows(key, part):
    chosen = slot_table(jax.random.fold_in(key, 5), FB_DEV * RATIO * CB_DEV, CAP_P, N_ROW * N_COL)
    return (chosen // CB_DEV).reshape(N_ROW, N_COL * CAP_P).astype(jnp.int32)


def draw_p_cols(key, part):
    chosen = slot_table(jax.random.fold_in(key, 5), FB_DEV * RATIO * CB_DEV, CAP_P, N_ROW * N_COL)
    return (chosen % CB_DEV).reshape(N_ROW, N_COL * CAP_P).astype(jnp.int32)


def draw_p_count(key, part):
    key = jax.random.fold_in(key, 12)
    lower = jax.random.randint(key, (N_ROW, N_COL), max(1, CAP_P // 2), CAP_P + 1)
    marked = (jnp.arange(N_ROW)[:, None] + jnp.arange(N_COL)[None, :]) % 3 == 0
    return jnp.where(marked, CAP_P, lower).astype(jnp.int32)


def steps_of(own_key, shape, shards, smallest, top_value):
    def one(position, blocks):
        steps = jax.random.uniform(jax.random.fold_in(jax.random.fold_in(own_key, 6), position), (blocks,), jnp.float32, smallest / len(shards), top_value / len(shards))
        return jnp.repeat(jnp.exp(steps), shape[position] // blocks).reshape((-1,) + (1,) * (len(shape) - position - 1))

    gain = one(*shards[0])
    for cut in shards[1:]:
        gain = gain * one(*cut)
    return gain


def bell_draw(own_key, dims, scale, bound, cuts=(), kind=jnp.bfloat16):
    result = scale * jax.random.normal(own_key, dims, jnp.float32)
    if cuts:
        result = result * steps_of(own_key, dims, cuts, -0.22, 0.18)
    return jnp.clip(result, -bound, bound).astype(kind)


def setup_inputs(seed: int = 0) -> dict:
    streams_of = jax.random.split(jax.random.key(seed), 9)
    a_values = bell_draw(streams_of[0], (N_COL, N_ROW * CAP_A, BS * BS), (72 * BS) ** -0.5, 0.09375, ((0, 32), (1, 8)))
    a_rows = draw_a_rows(jax.random.fold_in(streams_of[8], 71), 0)
    a_cols = draw_a_cols(jax.random.fold_in(streams_of[8], 71), 0)
    a_count = draw_a_count(jax.random.fold_in(streams_of[8], 71), 0)
    p_values = bell_draw(streams_of[4], (N_ROW, N_COL * CAP_P, BS * BS), 0.25, 1.5, ((0, 8), (1, 32)))
    p_rows = draw_p_rows(jax.random.fold_in(streams_of[8], 71), 0)
    p_cols = draw_p_cols(jax.random.fold_in(streams_of[8], 71), 0)
    p_count = draw_p_count(jax.random.fold_in(streams_of[8], 71), 0)
    return {"a_values": a_values, "a_rows": a_rows, "a_cols": a_cols, "a_count": a_count, "p_values": p_values, "p_rows": p_rows, "p_cols": p_cols, "p_count": p_count}


def live_blocks(values, count, slot_total):
    keep_mask = (jnp.arange(slot_total) < count).astype(values.dtype)
    return (values * keep_mask[:, None]).reshape(slot_total, BS, BS)


def reference(a_values, a_rows, a_cols, a_count, p_values, p_rows, p_cols, p_count):
    panel_rows = FB_DEV * RATIO
    p_tiles = p_values.reshape(N_ROW, N_COL, CAP_P, BS * BS)
    p_rows_t = p_rows.reshape(N_ROW, N_COL, CAP_P).astype(jnp.int32)
    p_cols_t = p_cols.reshape(N_ROW, N_COL, CAP_P).astype(jnp.int32) + (jnp.arange(N_COL, dtype=jnp.int32) * CB_DEV)[None, :, None]

    def prolong_panel(record):
        values, list_rows, list_cols, counts = record
        blocks = jax.vmap(lambda v, c: live_blocks(v, c, CAP_P))(values, counts)
        block_grid = jnp.zeros((panel_rows, NBC, BS, BS), values.dtype)
        block_grid = block_grid.at[list_rows.reshape(-1), list_cols.reshape(-1)].add(blocks.reshape(-1, BS, BS))
        return block_grid.transpose(0, 2, 1, 3).reshape(panel_rows, BS, NC)

    panels = lax.map(prolong_panel, (p_tiles, p_rows_t, p_cols_t, p_count))

    a_tiles = a_values.reshape(N_COL, N_ROW, CAP_A, BS * BS)
    a_rows_t = a_rows.reshape(N_COL, N_ROW, CAP_A).astype(jnp.int32)
    a_cols_t = a_cols.reshape(N_COL, N_ROW, CAP_A).astype(jnp.int32)

    def product_panel(record):
        values, list_rows, list_cols, counts = record
        running = jnp.zeros((FB_DEV, BS, NC), jnp.float32)
        for row_index in range(N_ROW):
            blocks = live_blocks(values[row_index], counts[row_index], CAP_A).astype(jnp.float32)
            picked = panels[row_index][list_cols[row_index]].astype(jnp.float32)
            running = running.at[list_rows[row_index]].add(jnp.einsum("kab,kbn->kan", blocks, picked))
        return running.astype(jnp.bfloat16)

    product = lax.map(product_panel, (a_tiles, a_rows_t, a_cols_t, a_count))
    product_blocks = product.reshape(NBF, BS, NC)

    fine_rows = (p_rows_t + (jnp.arange(N_ROW, dtype=jnp.int32) * panel_rows)[:, None, None]).reshape(-1, CAP_P)
    coarse_cols = p_cols_t.reshape(-1, CAP_P)
    counts_all = p_count.reshape(-1)
    tiles_all = p_tiles.reshape(-1, CAP_P, BS * BS)

    def add_tile(running, record):
        values, list_rows, list_cols, counts = record
        blocks = live_blocks(values, counts, CAP_P).astype(jnp.float32)
        picked = product_blocks[list_rows].astype(jnp.float32)
        return running.at[list_cols].add(jnp.einsum("kab,kan->kbn", blocks, picked)), None

    coarse, _ = lax.scan(add_tile, jnp.zeros((NBC, BS, NC), jnp.float32), (tiles_all, fine_rows, coarse_cols, counts_all))
    return coarse.reshape(NC, NC)
```

```python
import functools

import jax
import jax.numpy as jnp
from jax import lax
from jax.experimental import pallas as pl
from jax.experimental.pallas import tpu as pltpu
from jax.sharding import PartitionSpec as P

BS = 64
FB_DEV = 4
CB_DEV = 2
Q = 4
SLOTS_A = 16
SLOTS_P = 4
PAIRS_A = SLOTS_A // 2
PAIRS_P = SLOTS_P // 2
LANES = 2 * BS
KEYS = 16
A_ROWS = PAIRS_A * BS + KEYS + SLOTS_A
P_ROWS = PAIRS_P * BS + KEYS
FINE = FB_DEV * BS
HALF = 2 * CB_DEV * BS
MESH = pl.DeviceIdType.MESH
BF16 = jnp.bfloat16
F32 = jnp.float32


def remote(src, dst, send, recv, target):
    return pltpu.make_async_remote_copy(
        src_ref=src, dst_ref=dst, send_sem=send, recv_sem=recv, device_id=target, device_id_type=MESH
    )


def swap_halves(x):
    return jnp.concatenate([x[:, BS:], x[:, :BS]], axis=1)


def tile_rows(row):
    return jnp.broadcast_to(row, (16, LANES)).astype(BF16)


def scaled(x, mask):
    return (x.reshape(BS // 16, 16, LANES) * mask[None]).reshape(BS, LANES)


def kernel(
    nr,
    ar, ac, an, pr, pc, pn, a_ref, p_ref, out_ref,
    abuf, zbuf, cbuf, tbuf, gbuf, left, rhs, restrict, acc, prod, outgoing, incoming, own,
    zs, zr, cs, cr, asnd, arcv, afs, afr, b2s, b2r, c2s, c2r, b3s, b3r, pgs, pgr, fs, fr,
):
    ny = nr // 2
    i = lax.axis_index("row")
    j = lax.axis_index("col")
    z, q = j // Q, j % Q
    xl, y = i // ny, i % ny
    mate = (1 - xl) * ny + y
    twin = q + 1 - 2 * (q % 2)
    far = (q + 2) % Q
    far_twin = (twin + 2) % Q
    at = lambda row, zz, qq: (row, zz * Q + qq)
    hop = lambda k, d: (k + d) % nr

    barrier = pltpu.get_barrier_semaphore()
    for d in range(1, nr):
        pl.semaphore_signal(barrier, inc=1, device_id=at(hop(i, d), z, q), device_id_type=MESH)
        pl.semaphore_signal(barrier, inc=1, device_id=at(i, hop(z, d), q), device_id_type=MESH)
    pl.semaphore_signal(barrier, inc=1, device_id=at(i, z, twin), device_id_type=MESH)
    pl.semaphore_signal(barrier, inc=1, device_id=at(i, z, far), device_id_type=MESH)

    lane = lax.broadcasted_iota(jnp.int32, (1, LANES), 1)
    second = lane >= BS
    half = second.astype(jnp.int32)
    rows_u = lax.broadcasted_iota(jnp.int32, (KEYS, LANES), 0)
    rows_s = lax.broadcasted_iota(jnp.int32, (SLOTS_A, LANES), 0)
    half_s = (lax.broadcasted_iota(jnp.int32, (SLOTS_A, LANES), 1) >= BS).astype(jnp.int32)
    p_keys = jnp.full((KEYS, LANES), -1, jnp.int32)
    for u in range(PAIRS_P):
        keys = [
            jnp.where(s < pn[0, 0], pr[0, s] * CB_DEV + pc[0, s], -1) for s in (2 * u, 2 * u + 1)
        ]
        p_keys = jnp.where(rows_u == u, jnp.where(second, keys[1], keys[0]), p_keys)
    tile = jnp.concatenate([p_ref[...], p_keys.astype(F32).astype(BF16)], axis=0)
    zbuf[z] = tile
    cbuf[i] = tile
    a_keys = jnp.full((KEYS, LANES), -1, jnp.int32)
    for u in range(PAIRS_A):
        keys = [jnp.where(s < an[0, 0], ar[0, s], -1) for s in (2 * u, 2 * u + 1)]
        a_keys = jnp.where(rows_u == u, jnp.where(second, keys[1], keys[0]), a_keys)
    a_cols = jnp.zeros((SLOTS_A, LANES), jnp.int32)
    for s in range(SLOTS_A):
        a_cols = jnp.where(rows_s == s, ac[0, s], a_cols)
    a_cols = a_cols * 2 + half_s
    abuf[i] = jnp.concatenate(
        [a_ref[...], a_keys.astype(F32).astype(BF16), a_cols.astype(F32).astype(BF16)], axis=0
    )

    pl.semaphore_wait(barrier, 2 * (nr - 1) + 2)

    sent = []

    def send(*args):
        copy = remote(*args)
        copy.start()
        sent.append(copy)

    for d in range(1, nr):
        to = hop(z, d)
        send(zbuf.at[z], zbuf.at[z], zs.at[to], zr.at[z], at(i, to, q))
    for d in range(1, nr):
        to = hop(i, d)
        send(cbuf.at[i], cbuf.at[i], cs.at[to], cr.at[i], at(to, z, q))
    send(abuf.at[i], abuf.at[i], asnd.at[0], arcv.at[0], at(mate, z, q))
    for e in range(1, ny):
        send(abuf.at[i], abuf.at[i], asnd.at[e], arcv.at[e], at(xl * ny + (y + e) % ny, z, q))

    for d in range(nr):
        k = hop(z, nr - d)
        if d:
            remote(zbuf.at[k], zbuf.at[k], zs.at[k], zr.at[k], at(i, k, q)).wait_recv()

        @pl.when(k == i)
        def _():
            gbuf[q, i] = zbuf[i]

        @pl.when(k != i)
        def _():
            remote(zbuf.at[k], gbuf.at[q, i], b2s.at[k], b2r.at[i], at(k, z, q)).start()

    remote(abuf.at[mate], abuf.at[mate], asnd.at[0], arcv.at[0], at(mate, z, q)).wait_recv()
    for e in range(1, ny):
        send(abuf.at[mate], abuf.at[mate], afs.at[e], afr.at[e], at(xl * ny + (y + e) % ny, z, q))

    for d in range(nr):
        k = hop(i, nr - d)
        if d:
            remote(cbuf.at[k], cbuf.at[k], cs.at[k], cr.at[k], at(k, z, q)).wait_recv()

        @pl.when(k == z)
        def _():
            tbuf[z] = cbuf[z]

        @pl.when(k != z)
        def _():
            remote(cbuf.at[k], tbuf.at[z], c2s.at[k], c2r.at[z], at(i, k, q)).start()

    for d in range(nr):
        k = hop(i, nr - d)
        if d:
            remote(zbuf.at[k], gbuf.at[q, k], b2s.at[k], b2r.at[k], at(k, z, q)).wait_recv()
        send(gbuf.at[q, k], gbuf.at[q, k], b3s.at[0, k], b3r.at[0, k], at(i, z, far))
        send(gbuf.at[q, k], gbuf.at[q, k], b3s.at[1, k], b3r.at[1, k], at(i, z, twin))
    for d in range(nr):
        k = hop(i, nr - d)
        remote(gbuf.at[far, k], gbuf.at[far, k], b3s.at[0, k], b3r.at[0, k], at(i, z, far)).wait_recv()
        send(gbuf.at[far, k], gbuf.at[far, k], b3s.at[2, k], b3r.at[2, k], at(i, z, twin))

    for e in range(1, ny):
        k = xl * ny + (y + ny - e) % ny
        remote(abuf.at[k], abuf.at[k], asnd.at[e], arcv.at[e], at(k, z, q)).wait_recv()
    for e in range(1, ny):
        k = (1 - xl) * ny + (y + ny - e) % ny
        remote(abuf.at[k], abuf.at[k], afs.at[e], afr.at[e], at(k, z, q)).wait_recv()

    @pl.loop(0, nr)
    def _(k):
        keys = abuf[k, pl.ds(PAIRS_A * BS, KEYS)].astype(F32)
        for u in range(PAIRS_A):
            block = abuf[k, pl.ds(u * BS, BS)]
            for r in range(FB_DEV):
                mask = tile_rows((keys[u : u + 1] == r).astype(F32))
                left[k, pl.ds(r * BS, BS), pl.ds(u * LANES, LANES)] = scaled(block, mask)

    for d in range(1, nr):
        k = hop(z, d)
        remote(cbuf.at[k], tbuf.at[k], c2s.at[k], c2r.at[k], at(i, k, q)).wait_recv()

    def sources(tile):
        keys = tile[PAIRS_P * BS :].astype(F32)
        found = []
        for u in range(PAIRS_P):
            block = tile[u * BS : (u + 1) * BS]
            key = keys[u : u + 1]
            found += [(block, key), (swap_halves(block), swap_halves(key))]
        return found

    half_f = half.astype(F32)

    @pl.loop(0, nr)
    def _(k):
        found = sources(tbuf[k])
        for c in range(0, Q * FB_DEV, 2):
            strip = []
            for cc in (c, c + 1):
                total = jnp.zeros((BS, LANES), BF16)
                for block, key in found:
                    total += scaled(block, tile_rows((key == 2 * cc + half_f).astype(F32)))
                strip.append(total)
            square = jnp.concatenate(strip, axis=0).astype(F32)
            restrict[k, :, pl.ds(c * BS, LANES)] = square.T.astype(BF16)

    def multiply(first):
        acc[...] = jnp.zeros_like(acc)

        @pl.loop(0, nr)
        def _(k):
            cols = abuf[k, pl.ds(PAIRS_A * BS + KEYS, SLOTS_A)].astype(F32)
            for w in range(2):
                found = sources(gbuf[first + w, k])
                masks = [(cols == key).astype(F32) for _, key in found]
                for s in range(SLOTS_A):
                    total = jnp.zeros((BS, LANES), BF16)
                    for (block, _), mask in zip(found, masks):
                        total += scaled(block, tile_rows(mask[s : s + 1]))
                    rhs[pl.ds(s * BS, BS), pl.ds(w * LANES, LANES)] = total
            acc[...] += jnp.dot(left[k], rhs[...], preferred_element_type=F32)

    for h in range(2):
        side = q // 2 if h == 0 else 1 - q // 2
        for d in range(nr):
            k = hop(i, nr - d)
            if h == 0:
                remote(gbuf.at[twin, k], gbuf.at[twin, k], b3s.at[1, k], b3r.at[1, k], at(i, z, twin)).wait_recv()
            else:
                remote(
                    gbuf.at[far_twin, k], gbuf.at[far_twin, k], b3s.at[2, k], b3r.at[2, k], at(i, z, twin)
                ).wait_recv()
        multiply(2 * side)
        prod[q, side] = acc[...].astype(BF16)
        send(prod.at[q, side], prod.at[q, side], pgs.at[0, h], pgr.at[0, h], at(i, z, far))
        send(prod.at[q, side], prod.at[q, side], pgs.at[1, h], pgr.at[1, h], at(i, z, twin))
    for h in range(2):
        side = 1 - q // 2 if h == 0 else q // 2
        remote(prod.at[far, side], prod.at[far, side], pgs.at[0, h], pgr.at[0, h], at(i, z, far)).wait_recv()
        send(prod.at[far, side], prod.at[far, side], pgs.at[2, h], pgr.at[2, h], at(i, z, twin))
    for h in range(2):
        side = q // 2 if h == 0 else 1 - q // 2
        remote(prod.at[twin, side], prod.at[twin, side], pgs.at[1, h], pgr.at[1, h], at(i, z, twin)).wait_recv()
        remote(
            prod.at[far_twin, 1 - side], prod.at[far_twin, 1 - side], pgs.at[2, h], pgr.at[2, h], at(i, z, twin)
        ).wait_recv()

    def share(k, h):
        total = jnp.zeros((LANES, HALF), F32)
        for p in range(Q):
            total += jnp.dot(
                restrict[k, :, p * FINE : (p + 1) * FINE], prod[p, h], preferred_element_type=F32
            )
        return total

    order = sorted(range(1, nr), key=lambda d: -min(d, nr - d))
    for d in order:
        k = hop(z, d)

        @pl.loop(0, 2)
        def _(h):
            outgoing[k, h] = share(k, h).astype(BF16)

        send(outgoing.at[k], incoming.at[z], fs.at[k], fr.at[z], at(i, k, q))

    @pl.loop(0, 2)
    def _(h):
        own[h] = share(z, h)

    for d in reversed(order):
        k = hop(z, d)
        remote(outgoing.at[k], incoming.at[k], fs.at[k], fr.at[k], at(i, k, q)).wait_recv()
    for h in range(2):
        total = own[h]
        for d in range(1, nr):
            total += incoming[hop(z, d), h].astype(F32)
        out_ref[:, h * HALF : (h + 1) * HALF] = total

    for copy in sent:
        copy.wait_send()
    for k in range(nr):

        @pl.when(k != i)
        def _():
            remote(zbuf.at[k], gbuf.at[q, i], b2s.at[k], b2r.at[i], at(k, z, q)).wait_send()

        @pl.when(k != z)
        def _():
            remote(cbuf.at[k], tbuf.at[z], c2s.at[k], c2r.at[z], at(i, k, q)).wait_send()


def pairs(values, slots):
    blocks = values.reshape(slots // 2, 2, BS, BS)
    return blocks.transpose(0, 2, 1, 3).reshape(slots // 2 * BS, LANES)


def solution(mesh):
    nr = mesh.shape["row"]
    ny = nr // 2

    def shards(a_values, a_rows, a_cols, a_count, p_values, p_rows, p_cols, p_count):
        dma = lambda *n: pltpu.SemaphoreType.DMA(n)
        smem = pl.BlockSpec(memory_space=pltpu.SMEM)
        vmem = pl.BlockSpec(memory_space=pltpu.VMEM)
        lists = lambda n=1: pltpu.VMEM((n, nr, P_ROWS, LANES), BF16)
        return pl.pallas_call(
            functools.partial(kernel, nr),
            out_shape=jax.ShapeDtypeStruct((CB_DEV * BS, 2 * HALF), F32),
            in_specs=[smem] * 6 + [vmem] * 2,
            out_specs=vmem,
            scratch_shapes=[
                pltpu.VMEM((nr, A_ROWS, LANES), BF16),
                pltpu.VMEM((nr, P_ROWS, LANES), BF16),
                pltpu.VMEM((nr, P_ROWS, LANES), BF16),
                pltpu.VMEM((nr, P_ROWS, LANES), BF16),
                pltpu.VMEM((Q, nr, P_ROWS, LANES), BF16),
                pltpu.VMEM((nr, FINE, SLOTS_A * BS), BF16),
                pltpu.VMEM((SLOTS_A * BS, HALF), BF16),
                pltpu.VMEM((nr, LANES, Q * FINE), BF16),
                pltpu.VMEM((FINE, HALF), F32),
                pltpu.VMEM((Q, 2, FINE, HALF), BF16),
                pltpu.VMEM((nr, 2, LANES, HALF), BF16),
                pltpu.VMEM((nr, 2, LANES, HALF), BF16),
                pltpu.VMEM((2, LANES, HALF), F32),
                dma(nr), dma(nr), dma(nr), dma(nr),
                dma(ny), dma(ny), dma(ny), dma(ny),
                dma(nr), dma(nr), dma(nr), dma(nr),
                dma(3, nr), dma(3, nr),
                dma(3, 2), dma(3, 2),
                dma(nr), dma(nr),
            ],
            compiler_params=pltpu.CompilerParams(
                collective_id=0, has_side_effects=True, vmem_limit_bytes=40 * 2**20
            ),
        )(
            a_rows, a_cols, a_count, p_rows, p_cols, p_count,
            pairs(a_values[0], SLOTS_A), pairs(p_values[0], SLOTS_P),
        )

    return jax.shard_map(
        shards,
        mesh=mesh,
        in_specs=(
            P("col", "row", None),
            P("col", "row"),
            P("col", "row"),
            P("col", "row"),
            P("row", "col", None),
            P("row", "col"),
            P("row", "col"),
            P("row", "col"),
        ),
        out_specs=P("col", "row"),
        check_vma=False,
    )
```

```python
import functools

import jax
import jax.numpy as jnp
from jax import lax
from jax.experimental import pallas as pl
from jax.experimental.pallas import tpu as pltpu
from jax.sharding import PartitionSpec as P

BS = 64
FB_DEV = 4
CB_DEV = 2
Q = 4
SLOTS_A = 16
SLOTS_P = 4
PAIRS_A = SLOTS_A // 2
PAIRS_P = SLOTS_P // 2
LANES = 2 * BS
KEYS = 16
A_ROWS = PAIRS_A * BS + KEYS + SLOTS_A
P_ROWS = PAIRS_P * BS + KEYS
FINE = FB_DEV * BS
HALF = 2 * CB_DEV * BS
MESH = pl.DeviceIdType.MESH
BF16 = jnp.bfloat16
F32 = jnp.float32


def remote(src, dst, send, recv, target):
    return pltpu.make_async_remote_copy(
        src_ref=src, dst_ref=dst, send_sem=send, recv_sem=recv, device_id=target, device_id_type=MESH
    )


def swap_halves(x):
    return jnp.concatenate([x[:, BS:], x[:, :BS]], axis=1)


def tile_rows(row):
    return jnp.broadcast_to(row, (16, LANES)).astype(BF16)


def scaled(x, mask):
    return (x.reshape(BS // 16, 16, LANES) * mask[None]).reshape(BS, LANES)


def kernel(
    nr,
    ar, ac, an, pr, pc, pn, a_ref, p_ref, out_ref,
    flat, woven, abuf, zbuf, cbuf, tbuf, gbuf, left, rhs, restrict, acc, prod, outgoing, incoming, own_out, own_in, own,
    zs, zr, cs, cr, asnd, arcv, afs, afr, b2s, b2r, c2s, c2r, b3s, b3r, pgs, pgr, fs, fr, os, orc,
):
    ny = nr // 2
    i = lax.axis_index("row")
    j = lax.axis_index("col")
    z, q = j // Q, j % Q
    xl, y = i // ny, i % ny
    mate = (1 - xl) * ny + y
    upper = q // 2 == 1
    row_of = lambda k: jnp.where(upper, (k + ny) % nr, k)
    twin = q + 1 - 2 * (q % 2)
    far = (q + 2) % Q
    far_twin = (twin + 2) % Q
    at = lambda row, zz, qq: (row, zz * Q + qq)
    hop = lambda k, d: (k + d) % nr

    barrier = pltpu.get_barrier_semaphore()
    for d in range(1, nr):
        pl.semaphore_signal(barrier, inc=1, device_id=at(hop(i, d), z, q), device_id_type=MESH)
        pl.semaphore_signal(barrier, inc=1, device_id=at(i, hop(z, d), q), device_id_type=MESH)
    pl.semaphore_signal(barrier, inc=1, device_id=at(i, z, twin), device_id_type=MESH)
    pl.semaphore_signal(barrier, inc=1, device_id=at(mate, z, far), device_id_type=MESH)
    for d in {1, nr - 1}:
        pl.semaphore_signal(barrier, inc=1, device_id=at(mate, hop(z, d), q), device_id_type=MESH)

    lane = lax.broadcasted_iota(jnp.int32, (1, LANES), 1)
    second = lane >= BS
    def pack(ref, slots):
        for m in range(BS // 2):
            flat[pl.ds(m, slots, stride=BS // 2)] = ref[0, :, m * LANES : (m + 1) * LANES].astype(F32)
        for u in range(slots // 2):
            one = flat[pl.ds(u * BS, BS // 2)]
            two = flat[pl.ds(u * BS + BS // 2, BS // 2)]
            woven[pl.ds(u * BS, BS // 2, stride=2)] = jnp.where(second, swap_halves(two), one)
            woven[pl.ds(u * BS + 1, BS // 2, stride=2)] = jnp.where(second, two, swap_halves(one))
        return woven[pl.ds(0, slots // 2 * BS)].astype(BF16)

    half = second.astype(jnp.int32)
    rows_u = lax.broadcasted_iota(jnp.int32, (KEYS, LANES), 0)
    rows_s = lax.broadcasted_iota(jnp.int32, (SLOTS_A, LANES), 0)
    half_s = (lax.broadcasted_iota(jnp.int32, (SLOTS_A, LANES), 1) >= BS).astype(jnp.int32)
    p_keys = jnp.full((KEYS, LANES), -1, jnp.int32)
    for u in range(PAIRS_P):
        keys = [
            jnp.where(s < pn[0, 0], pr[0, s] * CB_DEV + pc[0, s], -1) for s in (2 * u, 2 * u + 1)
        ]
        p_keys = jnp.where(rows_u == u, jnp.where(second, keys[1], keys[0]), p_keys)
    tile = jnp.concatenate([pack(p_ref, SLOTS_P), p_keys.astype(F32).astype(BF16)], axis=0)
    zbuf[z] = tile
    cbuf[i] = tile
    a_keys = jnp.full((KEYS, LANES), -1, jnp.int32)
    for u in range(PAIRS_A):
        keys = [jnp.where(s < an[0, 0], ar[0, s], -1) for s in (2 * u, 2 * u + 1)]
        a_keys = jnp.where(rows_u == u, jnp.where(second, keys[1], keys[0]), a_keys)
    a_cols = jnp.zeros((SLOTS_A, LANES), jnp.int32)
    for s in range(SLOTS_A):
        a_cols = jnp.where(rows_s == s, ac[0, s], a_cols)
    a_cols = a_cols * 2 + half_s
    abuf[i] = jnp.concatenate(
        [pack(a_ref, SLOTS_A), a_keys.astype(F32).astype(BF16), a_cols.astype(F32).astype(BF16)], axis=0
    )

    pl.semaphore_wait(barrier, 2 * (nr - 1) + 2 + len({1, nr - 1}))

    sent = []

    def send(*args):
        copy = remote(*args)
        copy.start()
        sent.append(copy)

    for d in range(1, nr):
        to = hop(z, d)
        send(zbuf.at[z], zbuf.at[z], zs.at[to], zr.at[z], at(i, to, q))
    for d in range(1, nr):
        to = hop(i, d)
        send(cbuf.at[i], cbuf.at[i], cs.at[to], cr.at[i], at(to, z, q))
    send(abuf.at[i], abuf.at[i], asnd.at[0], arcv.at[0], at(mate, z, q))
    for e in range(1, ny):
        send(abuf.at[i], abuf.at[i], asnd.at[e], arcv.at[e], at(xl * ny + (y + e) % ny, z, q))

    for d in range(nr):
        k = hop(z, nr - d)
        if d:
            remote(zbuf.at[k], zbuf.at[k], zs.at[k], zr.at[k], at(i, k, q)).wait_recv()

        to = row_of(k)

        @pl.when(to == i)
        def _():
            gbuf[q, i] = zbuf[k]

        @pl.when(to != i)
        def _():
            remote(zbuf.at[k], gbuf.at[q, i], b2s.at[k], b2r.at[i], at(to, z, q)).start()

    remote(abuf.at[mate], abuf.at[mate], asnd.at[0], arcv.at[0], at(mate, z, q)).wait_recv()
    for e in range(1, ny):
        send(abuf.at[mate], abuf.at[mate], afs.at[e], afr.at[e], at(xl * ny + (y + e) % ny, z, q))

    for d in range(nr):
        k = hop(i, nr - d)
        if d:
            remote(cbuf.at[k], cbuf.at[k], cs.at[k], cr.at[k], at(k, z, q)).wait_recv()

        @pl.when(k == z)
        def _():
            tbuf[z] = cbuf[z]

        @pl.when(k != z)
        def _():
            remote(cbuf.at[k], tbuf.at[z], c2s.at[k], c2r.at[z], at(i, k, q)).start()

    for d in range(nr):
        k = hop(i, nr - d)
        if d:
            remote(zbuf.at[k], gbuf.at[q, k], b2s.at[k], b2r.at[k], at(k, z, q)).wait_recv()
        send(gbuf.at[q, k], gbuf.at[q, k], b3s.at[0, k], b3r.at[0, k], at(mate, z, far))
        send(gbuf.at[q, k], gbuf.at[q, k], b3s.at[1, k], b3r.at[1, k], at(i, z, twin))
    for e in range(1, ny):
        k = xl * ny + (y + ny - e) % ny
        remote(abuf.at[k], abuf.at[k], asnd.at[e], arcv.at[e], at(k, z, q)).wait_recv()
    for e in range(1, ny):
        k = (1 - xl) * ny + (y + ny - e) % ny
        remote(abuf.at[k], abuf.at[k], afs.at[e], afr.at[e], at(k, z, q)).wait_recv()

    @pl.loop(0, nr)
    def _(k):
        keys = abuf[k, pl.ds(PAIRS_A * BS, KEYS)].astype(F32)
        for u in range(PAIRS_A):
            block = abuf[k, pl.ds(u * BS, BS)]
            for r in range(FB_DEV):
                mask = tile_rows((keys[u : u + 1] == r).astype(F32))
                left[k, pl.ds(r * BS, BS), pl.ds(u * LANES, LANES)] = scaled(block, mask)

    for d in range(1, nr):
        k = hop(z, d)
        remote(cbuf.at[k], tbuf.at[k], c2s.at[k], c2r.at[k], at(i, k, q)).wait_recv()

    def sources(tile):
        keys = tile[PAIRS_P * BS :].astype(F32)
        found = []
        for u in range(PAIRS_P):
            block = tile[u * BS : (u + 1) * BS]
            key = keys[u : u + 1]
            found += [(block, key), (swap_halves(block), swap_halves(key))]
        return found

    half_f = half.astype(F32)

    @pl.loop(0, nr)
    def _(k):
        found = sources(tbuf[k])
        for c in range(0, Q * FB_DEV, 2):
            strip = []
            for cc in (c, c + 1):
                total = jnp.zeros((BS, LANES), BF16)
                for block, key in found:
                    total += scaled(block, tile_rows((key == 2 * cc + half_f).astype(F32)))
                strip.append(total)
            square = jnp.concatenate(strip, axis=0).astype(F32)
            restrict[k, :, pl.ds(c * BS, LANES)] = square.T.astype(BF16)

    def multiply(first, k):
        cols = abuf[k, pl.ds(PAIRS_A * BS + KEYS, SLOTS_A)].astype(F32)
        for w in range(2):
            found = sources(gbuf[first + w, k])
            masks = [(cols == key).astype(F32) for _, key in found]
            for s in range(SLOTS_A):
                total = jnp.zeros((BS, LANES), BF16)
                for (block, _), mask in zip(found, masks):
                    total += scaled(block, tile_rows(mask[s : s + 1]))
                rhs[pl.ds(s * BS, BS), pl.ds(w * LANES, LANES)] = total
        acc[...] += jnp.dot(left[k], rhs[...], preferred_element_type=F32)

    from_far = lambda k: remote(gbuf.at[far, k], gbuf.at[far, k], b3s.at[0, k], b3r.at[0, k], at(mate, z, far))
    from_twin = lambda p, s, k: remote(gbuf.at[p, k], gbuf.at[p, k], b3s.at[s, k], b3r.at[s, k], at(i, z, twin))
    for h in range(2):
        side = q // 2 if h == 0 else 1 - q // 2
        acc[...] = jnp.zeros_like(acc)

        @pl.loop(0, nr)
        def _(d):
            k = hop(i, nr - d)
            if h == 0:
                from_far(k).wait_recv()
                from_twin(far, 2, k).start()
                from_twin(twin, 1, k).wait_recv()
            else:
                from_twin(far_twin, 2, k).wait_recv()
            multiply(2 * side, k)

        prod[q, side] = acc[...].astype(BF16)
        send(prod.at[q, side], prod.at[q, side], pgs.at[0, h], pgr.at[0, h], at(mate, z, far))
        send(prod.at[q, side], prod.at[q, side], pgs.at[1, h], pgr.at[1, h], at(i, z, twin))
    for h in range(2):
        side = 1 - q // 2 if h == 0 else q // 2
        remote(prod.at[far, side], prod.at[far, side], pgs.at[0, h], pgr.at[0, h], at(mate, z, far)).wait_recv()
        send(prod.at[far, side], prod.at[far, side], pgs.at[2, h], pgr.at[2, h], at(i, z, twin))
    for h in range(2):
        side = q // 2 if h == 0 else 1 - q // 2
        remote(prod.at[twin, side], prod.at[twin, side], pgs.at[1, h], pgr.at[1, h], at(i, z, twin)).wait_recv()
        remote(
            prod.at[far_twin, 1 - side], prod.at[far_twin, 1 - side], pgs.at[2, h], pgr.at[2, h], at(i, z, twin)
        ).wait_recv()

    def share(k, h):
        total = jnp.zeros((LANES, HALF), F32)
        for p in range(Q):
            total += jnp.dot(
                restrict[k, :, p * FINE : (p + 1) * FINE], prod[p, h], preferred_element_type=F32
            )
        return total

    half_way = nr // 2
    home = row_of(i)

    def leg(way, t, h):
        to = hop(z, 1 if way == 0 else nr - 1)
        row = home if t == half_way - 1 else i
        return remote(outgoing.at[way, t, h], incoming.at[way, t, h], fs.at[way, t, h], fr.at[way, t, h], at(row, to, q))

    for t in range(half_way):
        for other in (True, False):
            for way in range(2):
                h = 1 - way if other else way
                if t == 0 and other:
                    continue
                far_z = hop(z, half_way - t if way == 0 else nr - half_way + t)
                total = share(far_z, h)
                if t > 1 or (t == 1 and not other):
                    leg(way, t - 1, h).wait_recv()
                    total += incoming[way, t - 1, h].astype(F32)
                outgoing[way, t, h] = total.astype(BF16)
                copy = leg(way, t, h)
                copy.start()
                sent.append(copy)
        if t == 0:
            for h in range(2):
                own[h] = share(z, h)

            @pl.when(upper)
            def _():
                own_out[...] = own[...].astype(BF16)
                remote(own_out, own_in, os, orc, at(mate, z, q)).start()

    @pl.when(upper)
    def _():
        remote(own_out, own_in, os, orc, at(mate, z, q)).wait()
        own[...] = own_in[...].astype(F32)

    for h in range(2):
        total = own[h]
        for way in range(2):
            if half_way == 1 and h != way:
                continue
            leg(way, half_way - 1, h).wait_recv()
            total += incoming[way, half_way - 1, h].astype(F32)
        out_ref[:, h * HALF : (h + 1) * HALF] = total

    for copy in sent:
        copy.wait_send()
    for k in range(nr):
        from_twin(far, 2, k).wait_send()

        @pl.when(row_of(k) != i)
        def _():
            remote(zbuf.at[k], gbuf.at[q, i], b2s.at[k], b2r.at[i], at(row_of(k), z, q)).wait_send()

        @pl.when(k != z)
        def _():
            remote(cbuf.at[k], tbuf.at[z], c2s.at[k], c2r.at[z], at(i, k, q)).wait_send()


def solution(mesh):
    nr = mesh.shape["row"]
    ny = nr // 2

    def shards(a_values, a_rows, a_cols, a_count, p_values, p_rows, p_cols, p_count):
        dma = lambda *n: pltpu.SemaphoreType.DMA(n)
        smem = pl.BlockSpec(memory_space=pltpu.SMEM)
        vmem = pl.BlockSpec(memory_space=pltpu.VMEM)
        lists = lambda n=1: pltpu.VMEM((n, nr, P_ROWS, LANES), BF16)
        return pl.pallas_call(
            functools.partial(kernel, nr),
            out_shape=jax.ShapeDtypeStruct((CB_DEV * BS, 2 * HALF), F32),
            in_specs=[smem] * 6 + [vmem] * 2,
            out_specs=vmem,
            scratch_shapes=[
                pltpu.VMEM((SLOTS_A * BS // 2, LANES), F32),
                pltpu.VMEM((SLOTS_A * BS // 2, LANES), F32),
                pltpu.VMEM((nr, A_ROWS, LANES), BF16),
                pltpu.VMEM((nr, P_ROWS, LANES), BF16),
                pltpu.VMEM((nr, P_ROWS, LANES), BF16),
                pltpu.VMEM((nr, P_ROWS, LANES), BF16),
                pltpu.VMEM((Q, nr, P_ROWS, LANES), BF16),
                pltpu.VMEM((nr, FINE, SLOTS_A * BS), BF16),
                pltpu.VMEM((SLOTS_A * BS, HALF), BF16),
                pltpu.VMEM((nr, LANES, Q * FINE), BF16),
                pltpu.VMEM((FINE, HALF), F32),
                pltpu.VMEM((Q, 2, FINE, HALF), BF16),
                pltpu.VMEM((2, ny, 2, LANES, HALF), BF16),
                pltpu.VMEM((2, ny, 2, LANES, HALF), BF16),
                pltpu.VMEM((2, LANES, HALF), BF16),
                pltpu.VMEM((2, LANES, HALF), BF16),
                pltpu.VMEM((2, LANES, HALF), F32),
                dma(nr), dma(nr), dma(nr), dma(nr),
                dma(ny), dma(ny), dma(ny), dma(ny),
                dma(nr), dma(nr), dma(nr), dma(nr),
                dma(3, nr), dma(3, nr),
                dma(3, 2), dma(3, 2),
                dma(2, ny, 2), dma(2, ny, 2),
                pltpu.SemaphoreType.DMA, pltpu.SemaphoreType.DMA,
            ],
            compiler_params=pltpu.CompilerParams(
                collective_id=0, has_side_effects=True, vmem_limit_bytes=40 * 2**20
            ),
        )(
            a_rows, a_cols, a_count, p_rows, p_cols, p_count,
            a_values, p_values,
        )

    return jax.shard_map(
        shards,
        mesh=mesh,
        in_specs=(
            P("col", "row", None),
            P("col", "row"),
            P("col", "row"),
            P("col", "row"),
            P("row", "col", None),
            P("row", "col"),
            P("row", "col"),
            P("row", "col"),
        ),
        out_specs=P("col", "row"),
        check_vma=False,
    )
```

```python
import functools

import jax
import jax.numpy as jnp
from jax import lax
from jax.experimental import pallas as pl
from jax.experimental.pallas import tpu as pltpu
from jax.sharding import PartitionSpec as P

BS = 64
FB_DEV = 4
CB_DEV = 2
Q = 4
SLOTS_A = 16
SLOTS_P = 4
PAIRS_A = SLOTS_A // 2
PAIRS_P = SLOTS_P // 2
LANES = 2 * BS
KEYS = 16
A_ROWS = PAIRS_A * BS + KEYS + SLOTS_A
P_ROWS = PAIRS_P * BS + KEYS
FINE = FB_DEV * BS
HALF = 2 * CB_DEV * BS
MESH = pl.DeviceIdType.MESH
BF16 = jnp.bfloat16
F32 = jnp.float32


def remote(src, dst, send, recv, target):
    return pltpu.make_async_remote_copy(
        src_ref=src, dst_ref=dst, send_sem=send, recv_sem=recv, device_id=target, device_id_type=MESH
    )


def swap_halves(x):
    return jnp.concatenate([x[:, BS:], x[:, :BS]], axis=1)


def spread(row):
    return jnp.broadcast_to(row, (BS, LANES)).astype(BF16)


def kernel(
    nr,
    ar_h, ac_h, an_h, pr_h, pc_h, pn_h, a_h, p_h, out_ref,
    ar, ac, an, pr, pc, pn, a_ref, p_ref, flat, woven, abuf, cbuf, tbuf, gbuf, left, rhs0, rhs1, restrict, acc, prod, outgoing, incoming, own_out, own_in, own,
    ins, zs, zr, cs, cr, asnd, arcv, ans, anr, afs, afr, c2s, c2r, b3s, b3r, pgs, pgr, fs, fr, os, orc,
):
    ny = nr // 2
    i = lax.axis_index("row")
    j = lax.axis_index("col")
    z, q = j // Q, j % Q
    xl, y = i // ny, i % ny
    mate = (1 - xl) * ny + y
    upper = q // 2 == 1
    row_of = lambda k: jnp.where(upper, (k + ny) % nr, k)
    twin = q + 1 - 2 * (q % 2)
    far = (q + 2) % Q
    far_twin = (twin + 2) % Q
    at = lambda row, zz, qq: (row, zz * Q + qq)
    hop = lambda k, d: (k + d) % nr

    barrier = pltpu.get_barrier_semaphore()
    for d in range(1, nr):
        pl.semaphore_signal(barrier, inc=1, device_id=at(hop(i, d), z, q), device_id_type=MESH)
        pl.semaphore_signal(barrier, inc=1, device_id=at(i, hop(z, d), q), device_id_type=MESH)
        pl.semaphore_signal(barrier, inc=1, device_id=at(hop(i, d), row_of(i), q), device_id_type=MESH)
    pl.semaphore_signal(barrier, inc=1, device_id=at(i, z, twin), device_id_type=MESH)
    pl.semaphore_signal(barrier, inc=1, device_id=at(mate, z, far), device_id_type=MESH)

    @pl.when(row_of(i) != z)
    def _():
        pl.semaphore_signal(barrier, inc=1, device_id=at(i, row_of(i), q), device_id_type=MESH)

    for d in {1, nr - 1}:
        pl.semaphore_signal(barrier, inc=1, device_id=at(mate, hop(z, d), q), device_id_type=MESH)

    loads = [
        pltpu.make_async_copy(src, dst, ins.at[n])
        for n, (src, dst) in enumerate(
            [(p_h, p_ref), (pr_h, pr), (pc_h, pc), (pn_h, pn), (a_h, a_ref), (ar_h, ar), (ac_h, ac), (an_h, an)]
        )
    ]
    for load in loads:
        load.start()

    lane = lax.broadcasted_iota(jnp.int32, (1, LANES), 1)
    second = lane >= BS

    def pack(ref, slots):
        for m in range(BS // 2):
            flat[pl.ds(m, slots, stride=BS // 2)] = ref[0, :, m * LANES : (m + 1) * LANES].astype(F32)
        for u in range(slots // 2):
            one = flat[pl.ds(u * BS, BS // 2)]
            two = flat[pl.ds(u * BS + BS // 2, BS // 2)]
            woven[pl.ds(u * BS, BS // 2, stride=2)] = jnp.where(second, swap_halves(two), one)
            woven[pl.ds(u * BS + 1, BS // 2, stride=2)] = jnp.where(second, two, swap_halves(one))
        return woven[pl.ds(0, slots // 2 * BS)].astype(BF16)

    half = second.astype(jnp.int32)
    rows_u = lax.broadcasted_iota(jnp.int32, (KEYS, LANES), 0)
    rows_s = lax.broadcasted_iota(jnp.int32, (SLOTS_A, LANES), 0)
    half_s = (lax.broadcasted_iota(jnp.int32, (SLOTS_A, LANES), 1) >= BS).astype(jnp.int32)
    for load in loads[:4]:
        load.wait()
    p_keys = jnp.full((KEYS, LANES), -1, jnp.int32)
    for u in range(PAIRS_P):
        keys = [
            jnp.where(s < pn[0, 0], pr[0, s] * CB_DEV + pc[0, s], -1) for s in (2 * u, 2 * u + 1)
        ]
        p_keys = jnp.where(rows_u == u, jnp.where(second, keys[1], keys[0]), p_keys)
    tile = jnp.concatenate([pack(p_ref, SLOTS_P), p_keys.astype(F32).astype(BF16)], axis=0)
    cbuf[i] = tile
    for load in loads[4:]:
        load.wait()
    a_keys = jnp.full((KEYS, LANES), -1, jnp.int32)
    for u in range(PAIRS_A):
        keys = [jnp.where(s < an[0, 0], ar[0, s], -1) for s in (2 * u, 2 * u + 1)]
        a_keys = jnp.where(rows_u == u, jnp.where(second, keys[1], keys[0]), a_keys)
    a_cols = jnp.zeros((SLOTS_A, LANES), jnp.int32)
    for s in range(SLOTS_A):
        a_cols = jnp.where(rows_s == s, ac[0, s], a_cols)
    a_cols = a_cols * 2 + half_s
    abuf[i] = jnp.concatenate(
        [pack(a_ref, SLOTS_A), a_keys.astype(F32).astype(BF16), a_cols.astype(F32).astype(BF16)], axis=0
    )

    here = row_of(z) == i
    pl.semaphore_wait(barrier, 3 * nr + len({1, nr - 1}) - here.astype(jnp.int32))

    sent = []

    def send(*args):
        copy = remote(*args)
        copy.start()
        sent.append(copy)

    p_copy = lambda d: remote(
        cbuf.at[i], gbuf.at[q, i], zs.at[d], zr.at[i], at(row_of(z), hop(z, d), q)
    )
    away = sorted(range(1, nr), key=lambda d: -min(d, nr - d))
    for d in away:
        p_copy(d).start()

    @pl.when(here)
    def _():
        gbuf[q, i] = cbuf[i]

    @pl.when(jnp.logical_not(here))
    def _():
        p_copy(0).start()

    line = lambda e: xl * ny + (y + e) % ny
    cross = lambda e: (1 - xl) * ny + (y + e) % ny
    opposite = ny // 2
    a_mate = lambda s, k: remote(abuf.at[k], abuf.at[k], asnd.at[s], arcv.at[s], at(mate, z, q))
    a_line = lambda e, k: remote(abuf.at[k], abuf.at[k], ans.at[e], anr.at[e], at(line(e), z, q))
    a_next = lambda e, k: remote(abuf.at[k], abuf.at[k], afs.at[e], afr.at[e], at(line(e), z, q))

    def launch(copy):
        copy.start()
        sent.append(copy)

    launch(a_mate(0, i))
    for e in range(1, ny):
        launch(a_line(e, i))

    for d in range(1, nr):
        to = hop(i, d)
        send(cbuf.at[i], cbuf.at[i], cs.at[to], cr.at[i], at(to, z, q))

    a_mate(0, mate).wait_recv()
    for e in range(1, ny):
        if e != opposite:
            launch(a_next(e, mate))
    if opposite:
        a_line(opposite, line(opposite)).wait_recv()
        launch(a_mate(1, line(opposite)))

    for d in range(nr):
        k = hop(i, nr - d)

        @pl.when(jnp.logical_not((k == i) & here))
        def _():
            remote(cbuf.at[i], gbuf.at[q, k], zs.at[0], zr.at[k], at(k, row_of(i), q)).wait_recv()

        send(gbuf.at[q, k], gbuf.at[q, k], b3s.at[0, k], b3r.at[0, k], at(mate, z, far))
        send(gbuf.at[q, k], gbuf.at[q, k], b3s.at[1, k], b3r.at[1, k], at(i, z, twin))

    def sources(tile):
        keys = tile[PAIRS_P * BS :].astype(F32)
        found = []
        for u in range(PAIRS_P):
            block = tile[u * BS : (u + 1) * BS]
            key = keys[u : u + 1]
            found += [(block, spread(key)), (swap_halves(block), spread(swap_halves(key)))]
        return found

    def pick(found, wanted):
        total = jnp.zeros((BS, LANES), BF16)
        for block, key in found:
            total = jnp.where(key == wanted, block, total)
        return total

    def lay(first, k, rhs):
        cols = abuf[k, pl.ds(PAIRS_A * BS + KEYS, SLOTS_A)].astype(F32)
        for w in range(2):
            found = sources(gbuf[first + w, k])
            for s in range(SLOTS_A):
                rhs[pl.ds(s * BS, BS), pl.ds(w * LANES, LANES)] = pick(found, spread(cols[s : s + 1]))

    from_far = lambda k: remote(gbuf.at[far, k], gbuf.at[far, k], b3s.at[0, k], b3r.at[0, k], at(mate, z, far))
    from_twin = lambda p, s, k: remote(gbuf.at[p, k], gbuf.at[p, k], b3s.at[s, k], b3r.at[s, k], at(i, z, twin))

    def place(k):
        keys = abuf[k, pl.ds(PAIRS_A * BS, KEYS)].astype(F32)
        for u in range(PAIRS_A):
            block = abuf[k, pl.ds(u * BS, BS)]
            key = spread(keys[u : u + 1])
            for r in range(FB_DEV):
                left[k, pl.ds(r * BS, BS), pl.ds(u * LANES, LANES)] = jnp.where(key == r, block, 0).astype(BF16)

    def multiply(side, panels, arrived, fresh):
        for d in range(len(panels) + 1):
            if d < len(panels):
                arrived(panels[d])
                lay(2 * side, panels[d], (rhs0, rhs1)[d % 2])
            if d > 0:
                part = jnp.dot(left[panels[d - 1]], (rhs1, rhs0)[d % 2][...], preferred_element_type=F32)
                acc[...] = part if fresh and d == 1 else acc[...] + part

    def share_out(side, h):
        prod[q, side] = acc[...].astype(BF16)
        send(prod.at[q, side], prod.at[q, side], pgs.at[0, h], pgr.at[0, h], at(mate, z, far))
        send(prod.at[q, side], prod.at[q, side], pgs.at[1, h], pgr.at[1, h], at(i, z, twin))

    side = q // 2
    near = lambda k: from_twin(twin, 1, k).wait_recv()
    ours = [line(e) for e in range(ny)]
    theirs = [cross(e) for e in range(ny)]
    for e in range(1, ny):
        if e != opposite:
            a_line(e, line(e)).wait_recv()
    for k in ours:
        place(k)
    multiply(side, ours, near, True)
    for d in range(nr):
        k = hop(i, nr - d)
        from_far(k).wait_recv()
        from_twin(far, 2, k).start()

    for d in range(nr):
        k = hop(i, nr - d)
        if d:
            remote(cbuf.at[k], cbuf.at[k], cs.at[k], cr.at[k], at(k, z, q)).wait_recv()

        @pl.when(k == z)
        def _():
            tbuf[z] = cbuf[z]

        @pl.when(k != z)
        def _():
            remote(cbuf.at[k], tbuf.at[z], c2s.at[k], c2r.at[z], at(i, k, q)).start()

    for e in range(1, ny):
        if e != opposite:
            a_next(e, cross(e)).wait_recv()
    if opposite:
        a_mate(1, cross(opposite)).wait_recv()
    for k in theirs:
        place(k)
    multiply(side, theirs, near, False)
    share_out(side, 0)
    multiply(1 - side, ours + theirs, lambda k: from_twin(far_twin, 2, k).wait_recv(), True)
    share_out(1 - side, 1)

    for d in range(1, nr):
        k = hop(z, d)
        remote(cbuf.at[k], tbuf.at[k], c2s.at[k], c2r.at[k], at(i, k, q)).wait_recv()

    half_f = half.astype(F32)

    @pl.loop(0, nr)
    def _(k):
        found = sources(tbuf[k])
        for c in range(0, Q * FB_DEV, 2):
            strip = [pick(found, spread(2 * cc + half_f)) for cc in (c, c + 1)]
            square = jnp.concatenate(strip, axis=0).astype(F32)
            restrict[k, :, pl.ds(c * BS, LANES)] = square.T.astype(BF16)

    for h in range(2):
        side = 1 - q // 2 if h == 0 else q // 2
        remote(prod.at[far, side], prod.at[far, side], pgs.at[0, h], pgr.at[0, h], at(mate, z, far)).wait_recv()
        send(prod.at[far, side], prod.at[far, side], pgs.at[2, h], pgr.at[2, h], at(i, z, twin))
    for h in range(2):
        side = q // 2 if h == 0 else 1 - q // 2
        remote(prod.at[twin, side], prod.at[twin, side], pgs.at[1, h], pgr.at[1, h], at(i, z, twin)).wait_recv()
        remote(
            prod.at[far_twin, 1 - side], prod.at[far_twin, 1 - side], pgs.at[2, h], pgr.at[2, h], at(i, z, twin)
        ).wait_recv()

    def share(k, h):
        total = jnp.zeros((LANES, HALF), F32)
        for p in range(Q):
            total += jnp.dot(
                restrict[k, :, p * FINE : (p + 1) * FINE], prod[p, h], preferred_element_type=F32
            )
        return total

    half_way = nr // 2
    home = row_of(i)

    def leg(way, t, h):
        to = hop(z, 1 if way == 0 else nr - 1)
        row = home if t == half_way - 1 else i
        return remote(outgoing.at[way, t, h], incoming.at[way, t, h], fs.at[way, t, h], fr.at[way, t, h], at(row, to, q))

    for t in range(half_way):
        for other in (True, False):
            for way in range(2):
                h = 1 - way if other else way
                if t == 0 and other:
                    continue
                far_z = hop(z, half_way - t if way == 0 else nr - half_way + t)
                total = share(far_z, h)
                if t > 1 or (t == 1 and not other):
                    leg(way, t - 1, h).wait_recv()
                    total += incoming[way, t - 1, h].astype(F32)
                outgoing[way, t, h] = total.astype(BF16)
                copy = leg(way, t, h)
                copy.start()
                sent.append(copy)
        if t == 0:
            for h in range(2):
                own[h] = share(z, h)

            @pl.when(upper)
            def _():
                own_out[...] = own[...].astype(BF16)
                remote(own_out, own_in, os, orc, at(mate, z, q)).start()

    @pl.when(upper)
    def _():
        remote(own_out, own_in, os, orc, at(mate, z, q)).wait()
        own[...] = own_in[...].astype(F32)

    for h in range(2):
        total = own[h]
        for way in range(2):
            if half_way == 1 and h != way:
                continue
            leg(way, half_way - 1, h).wait_recv()
            total += incoming[way, half_way - 1, h].astype(F32)
        out_ref[:, h * HALF : (h + 1) * HALF] = total

    for copy in sent:
        copy.wait_send()
    for d in away:
        p_copy(d).wait_send()

    @pl.when(jnp.logical_not(here))
    def _():
        p_copy(0).wait_send()

    for k in range(nr):
        from_twin(far, 2, k).wait_send()

        @pl.when(k != z)
        def _():
            remote(cbuf.at[k], tbuf.at[z], c2s.at[k], c2r.at[z], at(i, k, q)).wait_send()


def solution(mesh):
    nr = mesh.shape["row"]
    ny = nr // 2

    def shards(a_values, a_rows, a_cols, a_count, p_values, p_rows, p_cols, p_count):
        dma = lambda *n: pltpu.SemaphoreType.DMA(n)
        vmem = pl.BlockSpec(memory_space=pltpu.VMEM)
        return pl.pallas_call(
            functools.partial(kernel, nr),
            out_shape=jax.ShapeDtypeStruct((CB_DEV * BS, 2 * HALF), F32),
            in_specs=[pl.BlockSpec(memory_space=pltpu.HBM)] * 8,
            out_specs=vmem,
            scratch_shapes=[
                pltpu.SMEM((1, SLOTS_A), jnp.int32),
                pltpu.SMEM((1, SLOTS_A), jnp.int32),
                pltpu.SMEM((1, 1), jnp.int32),
                pltpu.SMEM((1, SLOTS_P), jnp.int32),
                pltpu.SMEM((1, SLOTS_P), jnp.int32),
                pltpu.SMEM((1, 1), jnp.int32),
                pltpu.VMEM((1, SLOTS_A, BS * BS), BF16),
                pltpu.VMEM((1, SLOTS_P, BS * BS), BF16),
                pltpu.VMEM((SLOTS_A * BS // 2, LANES), F32),
                pltpu.VMEM((SLOTS_A * BS // 2, LANES), F32),
                pltpu.VMEM((nr, A_ROWS, LANES), BF16),
                pltpu.VMEM((nr, P_ROWS, LANES), BF16),
                pltpu.VMEM((nr, P_ROWS, LANES), BF16),
                pltpu.VMEM((Q, nr, P_ROWS, LANES), BF16),
                pltpu.VMEM((nr, FINE, SLOTS_A * BS), BF16),
                pltpu.VMEM((SLOTS_A * BS, HALF), BF16),
                pltpu.VMEM((SLOTS_A * BS, HALF), BF16),
                pltpu.VMEM((nr, LANES, Q * FINE), BF16),
                pltpu.VMEM((FINE, HALF), F32),
                pltpu.VMEM((Q, 2, FINE, HALF), BF16),
                pltpu.VMEM((2, ny, 2, LANES, HALF), BF16),
                pltpu.VMEM((2, ny, 2, LANES, HALF), BF16),
                pltpu.VMEM((2, LANES, HALF), BF16),
                pltpu.VMEM((2, LANES, HALF), BF16),
                pltpu.VMEM((2, LANES, HALF), F32),
                dma(8), dma(nr), dma(nr), dma(nr), dma(nr),
                dma(2), dma(2), dma(ny), dma(ny), dma(ny), dma(ny),
                dma(nr), dma(nr),
                dma(3, nr), dma(3, nr),
                dma(3, 2), dma(3, 2),
                dma(2, ny, 2), dma(2, ny, 2),
                pltpu.SemaphoreType.DMA, pltpu.SemaphoreType.DMA,
            ],
            compiler_params=pltpu.CompilerParams(
                collective_id=0, has_side_effects=True, vmem_limit_bytes=40 * 2**20
            ),
        )(
            a_rows, a_cols, a_count, p_rows, p_cols, p_count,
            a_values, p_values,
        )

    return jax.shard_map(
        shards,
        mesh=mesh,
        in_specs=(
            P("col", "row", None),
            P("col", "row"),
            P("col", "row"),
            P("col", "row"),
            P("row", "col", None),
            P("row", "col"),
            P("row", "col"),
            P("row", "col"),
        ),
        out_specs=P("col", "row"),
        check_vma=False,
    )
```

```python
import functools

import jax
import jax.numpy as jnp
from jax import lax
from jax.experimental import pallas as pl
from jax.experimental.pallas import tpu as pltpu
from jax.sharding import PartitionSpec as P

BS = 64
FB_DEV = 4
CB_DEV = 2
Q = 4
SLOTS_A = 16
SLOTS_P = 4
PAIRS_A = SLOTS_A // 2
PAIRS_P = SLOTS_P // 2
LANES = 2 * BS
KEYS = 16
A_ROWS = PAIRS_A * BS + KEYS + SLOTS_A
P_ROWS = PAIRS_P * BS + KEYS
FINE = FB_DEV * BS
HALF = 2 * CB_DEV * BS
MESH = pl.DeviceIdType.MESH
BF16 = jnp.bfloat16
F32 = jnp.float32


def remote(src, dst, send, recv, target):
    return pltpu.make_async_remote_copy(
        src_ref=src, dst_ref=dst, send_sem=send, recv_sem=recv, device_id=target, device_id_type=MESH
    )


def swap_halves(x):
    return jnp.concatenate([x[:, BS:], x[:, :BS]], axis=1)


def spread(row):
    return jnp.broadcast_to(row, (BS, LANES)).astype(BF16)


def kernel(
    nr,
    ar_h, ac_h, an_h, pr_h, pc_h, pn_h, a_h, p_h, out_ref,
    ar, ac, an, pr, pc, pn, a_ref, p_ref, flat, woven, abuf, cbuf, tbuf, gbuf, left, rhs0, rhs1, restrict, acc, prod, outgoing, incoming, held, own_out, own_in, own,
    ins, zs, zr, cs, cr, asnd, arcv, ans, anr, afs, afr, c2s, c2r, b3s, b3r, pgs, pgr, fs, fr, os, orc,
):
    ny = nr // 2
    i = lax.axis_index("row")
    j = lax.axis_index("col")
    z, q = j // Q, j % Q
    xl, y = i // ny, i % ny
    mate = (1 - xl) * ny + y
    upper = q // 2 == 1
    row_of = lambda k: jnp.where(upper, (k + ny) % nr, k)
    twin = q + 1 - 2 * (q % 2)
    far = (q + 2) % Q
    far_twin = (twin + 2) % Q
    at = lambda row, zz, qq: (row, zz * Q + qq)
    hop = lambda k, d: (k + d) % nr

    barrier = pltpu.get_barrier_semaphore()
    for d in range(1, nr):
        pl.semaphore_signal(barrier, inc=1, device_id=at(hop(i, d), z, q), device_id_type=MESH)
        pl.semaphore_signal(barrier, inc=1, device_id=at(i, hop(z, d), q), device_id_type=MESH)
        pl.semaphore_signal(barrier, inc=1, device_id=at(hop(i, d), row_of(i), q), device_id_type=MESH)
    pl.semaphore_signal(barrier, inc=1, device_id=at(i, z, twin), device_id_type=MESH)
    pl.semaphore_signal(barrier, inc=1, device_id=at(mate, z, far), device_id_type=MESH)

    @pl.when(row_of(i) != z)
    def _():
        pl.semaphore_signal(barrier, inc=1, device_id=at(i, row_of(i), q), device_id_type=MESH)

    for d in {1, nr - 1}:
        pl.semaphore_signal(barrier, inc=1, device_id=at(mate, hop(z, d), q), device_id_type=MESH)

    loads = [
        pltpu.make_async_copy(src, dst, ins.at[n])
        for n, (src, dst) in enumerate(
            [(p_h, p_ref), (pr_h, pr), (pc_h, pc), (pn_h, pn), (a_h, a_ref), (ar_h, ar), (ac_h, ac), (an_h, an)]
        )
    ]
    for load in loads:
        load.start()

    lane = lax.broadcasted_iota(jnp.int32, (1, LANES), 1)
    second = lane >= BS

    def pack(ref, slots):
        for m in range(BS // 2):
            flat[pl.ds(m, slots, stride=BS // 2)] = ref[0, :, m * LANES : (m + 1) * LANES].astype(F32)
        for u in range(slots // 2):
            one = flat[pl.ds(u * BS, BS // 2)]
            two = flat[pl.ds(u * BS + BS // 2, BS // 2)]
            woven[pl.ds(u * BS, BS // 2, stride=2)] = jnp.where(second, swap_halves(two), one)
            woven[pl.ds(u * BS + 1, BS // 2, stride=2)] = jnp.where(second, two, swap_halves(one))
        return woven[pl.ds(0, slots // 2 * BS)].astype(BF16)

    half = second.astype(jnp.int32)
    rows_u = lax.broadcasted_iota(jnp.int32, (KEYS, LANES), 0)
    rows_s = lax.broadcasted_iota(jnp.int32, (SLOTS_A, LANES), 0)
    half_s = (lax.broadcasted_iota(jnp.int32, (SLOTS_A, LANES), 1) >= BS).astype(jnp.int32)
    for load in loads[:4]:
        load.wait()
    p_keys = jnp.full((KEYS, LANES), -1, jnp.int32)
    for u in range(PAIRS_P):
        keys = [
            jnp.where(s < pn[0, 0], pr[0, s] * CB_DEV + pc[0, s], -1) for s in (2 * u, 2 * u + 1)
        ]
        p_keys = jnp.where(rows_u == u, jnp.where(second, keys[1], keys[0]), p_keys)
    tile = jnp.concatenate([pack(p_ref, SLOTS_P), p_keys.astype(F32).astype(BF16)], axis=0)
    cbuf[i] = tile
    for load in loads[4:]:
        load.wait()
    a_keys = jnp.full((KEYS, LANES), -1, jnp.int32)
    for u in range(PAIRS_A):
        keys = [jnp.where(s < an[0, 0], ar[0, s], -1) for s in (2 * u, 2 * u + 1)]
        a_keys = jnp.where(rows_u == u, jnp.where(second, keys[1], keys[0]), a_keys)
    a_cols = jnp.zeros((SLOTS_A, LANES), jnp.int32)
    for s in range(SLOTS_A):
        a_cols = jnp.where(rows_s == s, ac[0, s], a_cols)
    a_cols = a_cols * 2 + half_s
    abuf[i] = jnp.concatenate(
        [pack(a_ref, SLOTS_A), a_keys.astype(F32).astype(BF16), a_cols.astype(F32).astype(BF16)], axis=0
    )

    here = row_of(z) == i
    pl.semaphore_wait(barrier, 3 * nr + len({1, nr - 1}) - here.astype(jnp.int32))

    sent = []

    def send(*args):
        copy = remote(*args)
        copy.start()
        sent.append(copy)

    p_copy = lambda d: remote(
        cbuf.at[i], gbuf.at[q, i], zs.at[d], zr.at[i], at(row_of(z), hop(z, d), q)
    )
    away = sorted(range(1, nr), key=lambda d: -min(d, nr - d))
    for d in away:
        p_copy(d).start()

    @pl.when(here)
    def _():
        gbuf[q, i] = cbuf[i]

    @pl.when(jnp.logical_not(here))
    def _():
        p_copy(0).start()

    line = lambda e: xl * ny + (y + e) % ny
    cross = lambda e: (1 - xl) * ny + (y + e) % ny
    opposite = ny // 2
    a_mate = lambda s, k: remote(abuf.at[k], abuf.at[k], asnd.at[s], arcv.at[s], at(mate, z, q))
    a_line = lambda e, k: remote(abuf.at[k], abuf.at[k], ans.at[e], anr.at[e], at(line(e), z, q))
    a_next = lambda e, k: remote(abuf.at[k], abuf.at[k], afs.at[e], afr.at[e], at(line(e), z, q))

    def launch(copy):
        copy.start()
        sent.append(copy)

    launch(a_mate(0, i))
    for e in range(1, ny):
        launch(a_line(e, i))

    for d in range(1, nr):
        to = hop(i, d)
        send(cbuf.at[i], cbuf.at[i], cs.at[to], cr.at[i], at(to, z, q))

    a_mate(0, mate).wait_recv()
    for e in range(1, ny):
        if e != opposite:
            launch(a_next(e, mate))
    for d in range(nr):
        k = hop(i, nr - d)

        @pl.when(jnp.logical_not((k == i) & here))
        def _():
            remote(cbuf.at[i], gbuf.at[q, k], zs.at[0], zr.at[k], at(k, row_of(i), q)).wait_recv()

        send(gbuf.at[q, k], gbuf.at[q, k], b3s.at[0, k], b3r.at[0, k], at(mate, z, far))
        send(gbuf.at[q, k], gbuf.at[q, k], b3s.at[1, k], b3r.at[1, k], at(i, z, twin))

    def sources(tile):
        keys = tile[PAIRS_P * BS :].astype(F32)
        found = []
        for u in range(PAIRS_P):
            block = tile[u * BS : (u + 1) * BS]
            key = keys[u : u + 1]
            found += [(block, spread(key)), (swap_halves(block), spread(swap_halves(key)))]
        return found

    def pick(found, wanted):
        total = jnp.zeros((BS, LANES), BF16)
        for block, key in found:
            total = jnp.where(key == wanted, block, total)
        return total

    def lay(first, k, rhs):
        cols = abuf[k, pl.ds(PAIRS_A * BS + KEYS, SLOTS_A)].astype(F32)
        for w in range(2):
            found = sources(gbuf[first + w, k])
            for s in range(SLOTS_A):
                rhs[pl.ds(s * BS, BS), pl.ds(w * LANES, LANES)] = pick(found, spread(cols[s : s + 1]))

    if opposite:
        a_line(opposite, line(opposite)).wait_recv()
        launch(a_mate(1, line(opposite)))

    for d in range(nr):
        k = hop(i, nr - d)
        if d:
            remote(cbuf.at[k], cbuf.at[k], cs.at[k], cr.at[k], at(k, z, q)).wait_recv()

        @pl.when(k == z)
        def _():
            tbuf[z] = cbuf[z]

        @pl.when(k != z)
        def _():
            remote(cbuf.at[k], tbuf.at[z], c2s.at[k], c2r.at[z], at(i, k, q)).start()

    from_far = lambda k: remote(gbuf.at[far, k], gbuf.at[far, k], b3s.at[0, k], b3r.at[0, k], at(mate, z, far))
    from_twin = lambda p, s, k: remote(gbuf.at[p, k], gbuf.at[p, k], b3s.at[s, k], b3r.at[s, k], at(i, z, twin))

    def place(k):
        keys = abuf[k, pl.ds(PAIRS_A * BS, KEYS)].astype(F32)
        for u in range(PAIRS_A):
            block = abuf[k, pl.ds(u * BS, BS)]
            key = spread(keys[u : u + 1])
            for r in range(FB_DEV):
                left[k, pl.ds(r * BS, BS), pl.ds(u * LANES, LANES)] = jnp.where(key == r, block, 0).astype(BF16)

    def multiply(side, panels, arrived, fresh):
        for d in range(len(panels) + 1):
            if d < len(panels):
                arrived(panels[d])
                lay(2 * side, panels[d], (rhs0, rhs1)[d % 2])
            if d > 0:
                part = jnp.dot(left[panels[d - 1]], (rhs1, rhs0)[d % 2][...], preferred_element_type=F32)
                acc[...] = part if fresh and d == 1 else acc[...] + part

    def share_out(side, h):
        prod[q, side] = acc[...].astype(BF16)
        send(prod.at[q, side], prod.at[q, side], pgs.at[0, h], pgr.at[0, h], at(mate, z, far))
        send(prod.at[q, side], prod.at[q, side], pgs.at[1, h], pgr.at[1, h], at(i, z, twin))

    side = q // 2
    near = lambda k: from_twin(twin, 1, k).wait_recv()
    ours = [line(e) for e in range(ny)]
    theirs = [cross(e) for e in range(ny)]
    for e in range(1, ny):
        if e != opposite:
            a_line(e, line(e)).wait_recv()
    for k in ours:
        place(k)
    multiply(side, ours, near, True)
    for d in range(nr):
        k = hop(i, nr - d)
        from_far(k).wait_recv()
        from_twin(far, 2, k).start()

    for e in range(1, ny):
        if e != opposite:
            a_next(e, cross(e)).wait_recv()
    if opposite:
        a_mate(1, cross(opposite)).wait_recv()
    for k in theirs:
        place(k)
    multiply(side, theirs, near, False)
    share_out(side, 0)
    multiply(1 - side, ours + theirs, lambda k: from_twin(far_twin, 2, k).wait_recv(), True)
    share_out(1 - side, 1)

    for d in range(1, nr):
        k = hop(z, d)
        remote(cbuf.at[k], tbuf.at[k], c2s.at[k], c2r.at[k], at(i, k, q)).wait_recv()

    half_f = half.astype(F32)

    @pl.loop(0, nr)
    def _(k):
        found = sources(tbuf[k])
        for c in range(0, Q * FB_DEV, 2):
            strip = [pick(found, spread(2 * cc + half_f)) for cc in (c, c + 1)]
            square = jnp.concatenate(strip, axis=0).astype(F32)
            restrict[k, :, pl.ds(c * BS, LANES)] = square.T.astype(BF16)

    for h in range(2):
        side = 1 - q // 2 if h == 0 else q // 2
        remote(prod.at[far, side], prod.at[far, side], pgs.at[0, h], pgr.at[0, h], at(mate, z, far)).wait_recv()
        send(prod.at[far, side], prod.at[far, side], pgs.at[2, h], pgr.at[2, h], at(i, z, twin))
    for h in range(2):
        side = q // 2 if h == 0 else 1 - q // 2
        remote(prod.at[twin, side], prod.at[twin, side], pgs.at[1, h], pgr.at[1, h], at(i, z, twin)).wait_recv()
        remote(
            prod.at[far_twin, 1 - side], prod.at[far_twin, 1 - side], pgs.at[2, h], pgr.at[2, h], at(i, z, twin)
        ).wait_recv()

    def share(k, h):
        total = jnp.zeros((LANES, HALF), F32)
        for p in range(Q):
            total += jnp.dot(
                restrict[k, :, p * FINE : (p + 1) * FINE], prod[p, h], preferred_element_type=F32
            )
        return total

    half_way = nr // 2
    home = row_of(i)

    def leg(way, t, h, g):
        to = hop(z, 1 if way == 0 else nr - 1)
        row = home if t == half_way - 1 else i
        part = (way, t, h, pl.ds(g * BS, BS))
        return remote(
            outgoing.at[part], incoming.at[part], fs.at[way, t, h, g], fr.at[way, t, h, g], at(row, to, q)
        )

    for t in range(half_way):
        for other in (True, False):
            if t == 0 and other:
                continue
            for way in range(2):
                far_z = hop(z, half_way - t if way == 0 else nr - half_way + t)
                held[way] = share(far_z, 1 - way if other else way)
            for g in range(2):
                for way in range(2):
                    h = 1 - way if other else way
                    rows = pl.ds(g * BS, BS)
                    total = held[way, rows]
                    if t > 1 or (t == 1 and not other):
                        leg(way, t - 1, h, g).wait_recv()
                        total += incoming[way, t - 1, h, rows].astype(F32)
                    outgoing[way, t, h, rows] = total.astype(BF16)
                    launch(leg(way, t, h, g))
        if t == 0:
            for h in range(2):
                own[h] = share(z, h)

            @pl.when(upper)
            def _():
                own_out[...] = own[...].astype(BF16)
                remote(own_out, own_in, os, orc, at(mate, z, q)).start()

    @pl.when(upper)
    def _():
        remote(own_out, own_in, os, orc, at(mate, z, q)).wait()
        own[...] = own_in[...].astype(F32)

    for g in range(2):
        rows = pl.ds(g * BS, BS)
        for h in range(2):
            total = own[h, rows]
            for way in range(2):
                if half_way == 1 and h != way:
                    continue
                leg(way, half_way - 1, h, g).wait_recv()
                total += incoming[way, half_way - 1, h, rows].astype(F32)
            out_ref[rows, h * HALF : (h + 1) * HALF] = total

    for copy in sent:
        copy.wait_send()
    for d in away:
        p_copy(d).wait_send()

    @pl.when(jnp.logical_not(here))
    def _():
        p_copy(0).wait_send()

    for k in range(nr):
        from_twin(far, 2, k).wait_send()

        @pl.when(k != z)
        def _():
            remote(cbuf.at[k], tbuf.at[z], c2s.at[k], c2r.at[z], at(i, k, q)).wait_send()


def solution(mesh):
    nr = mesh.shape["row"]
    ny = nr // 2

    def shards(a_values, a_rows, a_cols, a_count, p_values, p_rows, p_cols, p_count):
        dma = lambda *n: pltpu.SemaphoreType.DMA(n)
        vmem = pl.BlockSpec(memory_space=pltpu.VMEM)
        return pl.pallas_call(
            functools.partial(kernel, nr),
            out_shape=jax.ShapeDtypeStruct((CB_DEV * BS, 2 * HALF), F32),
            in_specs=[pl.BlockSpec(memory_space=pltpu.HBM)] * 8,
            out_specs=vmem,
            scratch_shapes=[
                pltpu.SMEM((1, SLOTS_A), jnp.int32),
                pltpu.SMEM((1, SLOTS_A), jnp.int32),
                pltpu.SMEM((1, 1), jnp.int32),
                pltpu.SMEM((1, SLOTS_P), jnp.int32),
                pltpu.SMEM((1, SLOTS_P), jnp.int32),
                pltpu.SMEM((1, 1), jnp.int32),
                pltpu.VMEM((1, SLOTS_A, BS * BS), BF16),
                pltpu.VMEM((1, SLOTS_P, BS * BS), BF16),
                pltpu.VMEM((SLOTS_A * BS // 2, LANES), F32),
                pltpu.VMEM((SLOTS_A * BS // 2, LANES), F32),
                pltpu.VMEM((nr, A_ROWS, LANES), BF16),
                pltpu.VMEM((nr, P_ROWS, LANES), BF16),
                pltpu.VMEM((nr, P_ROWS, LANES), BF16),
                pltpu.VMEM((Q, nr, P_ROWS, LANES), BF16),
                pltpu.VMEM((nr, FINE, SLOTS_A * BS), BF16),
                pltpu.VMEM((SLOTS_A * BS, HALF), BF16),
                pltpu.VMEM((SLOTS_A * BS, HALF), BF16),
                pltpu.VMEM((nr, LANES, Q * FINE), BF16),
                pltpu.VMEM((FINE, HALF), F32),
                pltpu.VMEM((Q, 2, FINE, HALF), BF16),
                pltpu.VMEM((2, ny, 2, LANES, HALF), BF16),
                pltpu.VMEM((2, ny, 2, LANES, HALF), BF16),
                pltpu.VMEM((2, LANES, HALF), F32),
                pltpu.VMEM((2, LANES, HALF), BF16),
                pltpu.VMEM((2, LANES, HALF), BF16),
                pltpu.VMEM((2, LANES, HALF), F32),
                dma(8), dma(nr), dma(nr), dma(nr), dma(nr),
                dma(2), dma(2), dma(ny), dma(ny), dma(ny), dma(ny),
                dma(nr), dma(nr),
                dma(3, nr), dma(3, nr),
                dma(3, 2), dma(3, 2),
                dma(2, ny, 2, 2), dma(2, ny, 2, 2),
                pltpu.SemaphoreType.DMA, pltpu.SemaphoreType.DMA,
            ],
            compiler_params=pltpu.CompilerParams(
                collective_id=0, has_side_effects=True, vmem_limit_bytes=40 * 2**20
            ),
        )(
            a_rows, a_cols, a_count, p_rows, p_cols, p_count,
            a_values, p_values,
        )

    return jax.shard_map(
        shards,
        mesh=mesh,
        in_specs=(
            P("col", "row", None),
            P("col", "row"),
            P("col", "row"),
            P("col", "row"),
            P("row", "col", None),
            P("row", "col"),
            P("row", "col"),
            P("row", "col"),
        ),
        out_specs=P("col", "row"),
        check_vma=False,
    )
```

```python
import functools

import jax
import jax.numpy as jnp
from jax import lax
from jax.experimental import pallas as pl
from jax.experimental.pallas import tpu as pltpu
from jax.sharding import PartitionSpec as P

BS = 64
FB_DEV = 4
CB_DEV = 2
Q = 4
SLOTS_A = 16
SLOTS_P = 4
PAIRS_A = SLOTS_A // 2
PAIRS_P = SLOTS_P // 2
LANES = 2 * BS
KEYS = 16
A_ROWS = PAIRS_A * BS + KEYS + SLOTS_A
P_ROWS = PAIRS_P * BS + KEYS
FINE = FB_DEV * BS
HALF = 2 * CB_DEV * BS
MESH = pl.DeviceIdType.MESH
BF16 = jnp.bfloat16
F32 = jnp.float32


def remote(src, dst, send, recv, target):
    return pltpu.make_async_remote_copy(
        src_ref=src, dst_ref=dst, send_sem=send, recv_sem=recv, device_id=target, device_id_type=MESH
    )


def swap_halves(x):
    return jnp.concatenate([x[:, BS:], x[:, :BS]], axis=1)


def spread(row):
    return jnp.broadcast_to(row, (BS, LANES)).astype(BF16)


def kernel(
    nr,
    ar_h, ac_h, an_h, pr_h, pc_h, pn_h, a_h, p_h, out_ref,
    ar, ac, an, pr, pc, pn, a_ref, p_ref, flat, woven, abuf, cbuf, tbuf, gbuf, gkey, mykey, left, rhs0, rhs1, restrict, acc, prod, outgoing, incoming, held, own_out, own_in, own,
    ins, ks, kr, gs, gr, zs, zr, cs, cr, asnd, arcv, ans, anr, afs, afr, c2s, c2r, b3s, b3r, pgs, pgr, fs, fr, os, orc,
):
    ny = nr // 2
    i = lax.axis_index("row")
    j = lax.axis_index("col")
    z, q = j // Q, j % Q
    xl, y = i // ny, i % ny
    mate = (1 - xl) * ny + y
    upper = q // 2 == 1
    row_of = lambda k: jnp.where(upper, (k + ny) % nr, k)
    twin = q + 1 - 2 * (q % 2)
    far = (q + 2) % Q
    far_twin = (twin + 2) % Q
    at = lambda row, zz, qq: (row, zz * Q + qq)
    hop = lambda k, d: (k + d) % nr

    barrier = pltpu.get_barrier_semaphore()
    for d in range(1, nr):
        pl.semaphore_signal(barrier, inc=1, device_id=at(hop(i, d), z, q), device_id_type=MESH)
        pl.semaphore_signal(barrier, inc=1, device_id=at(i, hop(z, d), q), device_id_type=MESH)
        pl.semaphore_signal(barrier, inc=1, device_id=at(hop(i, d), row_of(i), q), device_id_type=MESH)
    pl.semaphore_signal(barrier, inc=1, device_id=at(i, z, twin), device_id_type=MESH)
    pl.semaphore_signal(barrier, inc=1, device_id=at(mate, z, far), device_id_type=MESH)

    @pl.when(row_of(i) != z)
    def _():
        pl.semaphore_signal(barrier, inc=1, device_id=at(i, row_of(i), q), device_id_type=MESH)

    for d in {1, nr - 1}:
        pl.semaphore_signal(barrier, inc=1, device_id=at(mate, hop(z, d), q), device_id_type=MESH)

    loads = [
        pltpu.make_async_copy(src, dst, ins.at[n])
        for n, (src, dst) in enumerate(
            [(p_h, p_ref), (pr_h, pr), (pc_h, pc), (pn_h, pn), (a_h, a_ref), (ar_h, ar), (ac_h, ac), (an_h, an)]
        )
    ]
    for load in loads:
        load.start()

    lane = lax.broadcasted_iota(jnp.int32, (1, LANES), 1)
    second = lane >= BS

    def pack(ref, slots):
        for m in range(BS // 2):
            flat[pl.ds(m, slots, stride=BS // 2)] = ref[0, :, m * LANES : (m + 1) * LANES].astype(F32)
        for u in range(slots // 2):
            one = flat[pl.ds(u * BS, BS // 2)]
            two = flat[pl.ds(u * BS + BS // 2, BS // 2)]
            woven[pl.ds(u * BS, BS // 2, stride=2)] = jnp.where(second, swap_halves(two), one)
            woven[pl.ds(u * BS + 1, BS // 2, stride=2)] = jnp.where(second, two, swap_halves(one))
        return woven[pl.ds(0, slots // 2 * BS)].astype(BF16)

    half = second.astype(jnp.int32)
    rows_u = lax.broadcasted_iota(jnp.int32, (KEYS, LANES), 0)
    rows_s = lax.broadcasted_iota(jnp.int32, (SLOTS_A, LANES), 0)
    half_s = (lax.broadcasted_iota(jnp.int32, (SLOTS_A, LANES), 1) >= BS).astype(jnp.int32)
    for load in loads[:4]:
        load.wait()
    p_keys = jnp.full((KEYS, LANES), -1, jnp.int32)
    for u in range(PAIRS_P):
        keys = [
            jnp.where(s < pn[0, 0], pr[0, s] * CB_DEV + pc[0, s], -1) for s in (2 * u, 2 * u + 1)
        ]
        p_keys = jnp.where(rows_u == u, jnp.where(second, keys[1], keys[0]), p_keys)
    tile = jnp.concatenate([pack(p_ref, SLOTS_P), p_keys.astype(F32).astype(BF16)], axis=0)
    cbuf[i] = tile
    mykey[...] = ((p_keys[0:1] + 1) + 64 * (p_keys[1:2] + 1)).astype(F32)
    for load in loads[4:]:
        load.wait()
    a_keys = jnp.full((KEYS, LANES), -1, jnp.int32)
    for u in range(PAIRS_A):
        keys = [jnp.where(s < an[0, 0], ar[0, s], -1) for s in (2 * u, 2 * u + 1)]
        a_keys = jnp.where(rows_u == u, jnp.where(second, keys[1], keys[0]), a_keys)
    a_cols = jnp.zeros((SLOTS_A, LANES), jnp.int32)
    for s in range(SLOTS_A):
        a_cols = jnp.where(rows_s == s, ac[0, s], a_cols)
    a_cols = a_cols * 2 + half_s
    abuf[i] = jnp.concatenate(
        [pack(a_ref, SLOTS_A), a_keys.astype(F32).astype(BF16), a_cols.astype(F32).astype(BF16)], axis=0
    )

    here = row_of(z) == i
    pl.semaphore_wait(barrier, 3 * nr + len({1, nr - 1}) - here.astype(jnp.int32))

    sent = []

    def send(*args):
        copy = remote(*args)
        copy.start()
        sent.append(copy)

    values = pl.ds(0, PAIRS_P * BS)
    p_copy = lambda d: remote(
        cbuf.at[i, values], gbuf.at[q, i], zs.at[d], zr.at[i], at(row_of(z), hop(z, d), q)
    )
    k_copy = lambda d: remote(mykey, gkey.at[q, i], ks.at[d], kr.at[i], at(row_of(z), hop(z, d), q))
    away = sorted(range(1, nr), key=lambda d: -min(d, nr - d))
    for d in away:
        k_copy(d).start()
        p_copy(d).start()

    @pl.when(here)
    def _():
        gbuf[q, i] = cbuf[i, values]
        gkey[q, i] = mykey[...]

    @pl.when(jnp.logical_not(here))
    def _():
        k_copy(0).start()
        p_copy(0).start()

    line = lambda e: xl * ny + (y + e) % ny
    cross = lambda e: (1 - xl) * ny + (y + e) % ny
    opposite = ny // 2
    a_mate = lambda s, k: remote(abuf.at[k], abuf.at[k], asnd.at[s], arcv.at[s], at(mate, z, q))
    a_line = lambda e, k: remote(abuf.at[k], abuf.at[k], ans.at[e], anr.at[e], at(line(e), z, q))
    a_next = lambda e, k: remote(abuf.at[k], abuf.at[k], afs.at[e], afr.at[e], at(line(e), z, q))

    def launch(copy):
        copy.start()
        sent.append(copy)

    launch(a_mate(0, i))
    for e in range(1, ny):
        launch(a_line(e, i))

    for d in range(1, nr):
        to = hop(i, d)
        send(cbuf.at[i], cbuf.at[i], cs.at[to], cr.at[i], at(to, z, q))

    a_mate(0, mate).wait_recv()
    for e in range(1, ny):
        if e != opposite:
            launch(a_next(e, mate))
    for d in range(nr):
        k = hop(i, nr - d)

        @pl.when(jnp.logical_not((k == i) & here))
        def _():
            remote(mykey, gkey.at[q, k], ks.at[0], kr.at[k], at(k, row_of(i), q)).wait_recv()
            remote(cbuf.at[i, values], gbuf.at[q, k], zs.at[0], zr.at[k], at(k, row_of(i), q)).wait_recv()

        send(gbuf.at[q, k], gbuf.at[q, k], b3s.at[0, k], b3r.at[0, k], at(mate, z, far))
        send(gbuf.at[q, k], gbuf.at[q, k], b3s.at[1, k], b3r.at[1, k], at(i, z, twin))

    def sources(tile, keys=None):
        keys = tile[PAIRS_P * BS :].astype(F32) if keys is None else keys
        found = []
        for u in range(PAIRS_P):
            block = tile[u * BS : (u + 1) * BS]
            key = keys[u : u + 1]
            found += [(block, spread(key)), (swap_halves(block), spread(swap_halves(key)))]
        return found

    def pick(found, wanted):
        total = jnp.zeros((BS, LANES), BF16)
        for block, key in found:
            total = jnp.where(key == wanted, block, total)
        return total

    def lay(first, k, rhs):
        cols = abuf[k, pl.ds(PAIRS_A * BS + KEYS, SLOTS_A)].astype(F32)
        for w in range(2):
            code = gkey[first + w, k]
            upper_key = jnp.floor(code * (1 / 64))
            found = sources(gbuf[first + w, k], jnp.concatenate([code - 64 * upper_key, upper_key], axis=0) - 1)
            for s in range(SLOTS_A):
                rhs[pl.ds(s * BS, BS), pl.ds(w * LANES, LANES)] = pick(found, spread(cols[s : s + 1]))

    launch(remote(gkey.at[q], gkey.at[q], gs.at[0], gr.at[0], at(mate, z, far)))
    launch(remote(gkey.at[q], gkey.at[q], gs.at[1], gr.at[1], at(i, z, twin)))
    if opposite:
        a_line(opposite, line(opposite)).wait_recv()
        launch(a_mate(1, line(opposite)))

    for d in range(nr):
        k = hop(i, nr - d)
        if d:
            remote(cbuf.at[k], cbuf.at[k], cs.at[k], cr.at[k], at(k, z, q)).wait_recv()

        @pl.when(k == z)
        def _():
            tbuf[z] = cbuf[z]

        @pl.when(k != z)
        def _():
            remote(cbuf.at[k], tbuf.at[z], c2s.at[k], c2r.at[z], at(i, k, q)).start()

    from_far = lambda k: remote(gbuf.at[far, k], gbuf.at[far, k], b3s.at[0, k], b3r.at[0, k], at(mate, z, far))
    from_twin = lambda p, s, k: remote(gbuf.at[p, k], gbuf.at[p, k], b3s.at[s, k], b3r.at[s, k], at(i, z, twin))

    def place(k):
        keys = abuf[k, pl.ds(PAIRS_A * BS, KEYS)].astype(F32)
        for u in range(PAIRS_A):
            block = abuf[k, pl.ds(u * BS, BS)]
            key = spread(keys[u : u + 1])
            for r in range(FB_DEV):
                left[k, pl.ds(r * BS, BS), pl.ds(u * LANES, LANES)] = jnp.where(key == r, block, 0).astype(BF16)

    def multiply(side, panels, arrived, fresh):
        for d in range(len(panels) + 1):
            if d < len(panels):
                arrived(panels[d])
                lay(2 * side, panels[d], (rhs0, rhs1)[d % 2])
            if d > 0:
                part = jnp.dot(left[panels[d - 1]], (rhs1, rhs0)[d % 2][...], preferred_element_type=F32)
                acc[...] = part if fresh and d == 1 else acc[...] + part

    def share_out(side, h):
        prod[q, side] = acc[...].astype(BF16)
        send(prod.at[q, side], prod.at[q, side], pgs.at[0, h], pgr.at[0, h], at(mate, z, far))
        send(prod.at[q, side], prod.at[q, side], pgs.at[1, h], pgr.at[1, h], at(i, z, twin))

    side = q // 2
    near = lambda k: from_twin(twin, 1, k).wait_recv()
    ours = [line(e) for e in range(ny)]
    theirs = [cross(e) for e in range(ny)]
    for e in range(1, ny):
        if e != opposite:
            a_line(e, line(e)).wait_recv()
    for k in ours:
        place(k)
    remote(gkey.at[twin], gkey.at[twin], gs.at[1], gr.at[1], at(i, z, twin)).wait_recv()
    multiply(side, ours, near, True)
    remote(gkey.at[far], gkey.at[far], gs.at[0], gr.at[0], at(mate, z, far)).wait_recv()
    launch(remote(gkey.at[far], gkey.at[far], gs.at[2], gr.at[2], at(i, z, twin)))
    for d in range(nr):
        k = hop(i, nr - d)
        from_far(k).wait_recv()
        from_twin(far, 2, k).start()

    for e in range(1, ny):
        if e != opposite:
            a_next(e, cross(e)).wait_recv()
    if opposite:
        a_mate(1, cross(opposite)).wait_recv()
    for k in theirs:
        place(k)
    multiply(side, theirs, near, False)
    share_out(side, 0)
    remote(gkey.at[far_twin], gkey.at[far_twin], gs.at[2], gr.at[2], at(i, z, twin)).wait_recv()
    multiply(1 - side, ours + theirs, lambda k: from_twin(far_twin, 2, k).wait_recv(), True)
    share_out(1 - side, 1)

    for d in range(1, nr):
        k = hop(z, d)
        remote(cbuf.at[k], tbuf.at[k], c2s.at[k], c2r.at[k], at(i, k, q)).wait_recv()

    half_f = half.astype(F32)

    @pl.loop(0, nr)
    def _(k):
        found = sources(tbuf[k])
        for c in range(0, Q * FB_DEV, 2):
            strip = [pick(found, spread(2 * cc + half_f)) for cc in (c, c + 1)]
            square = jnp.concatenate(strip, axis=0).astype(F32)
            restrict[k, :, pl.ds(c * BS, LANES)] = square.T.astype(BF16)

    for h in range(2):
        side = 1 - q // 2 if h == 0 else q // 2
        remote(prod.at[far, side], prod.at[far, side], pgs.at[0, h], pgr.at[0, h], at(mate, z, far)).wait_recv()
        send(prod.at[far, side], prod.at[far, side], pgs.at[2, h], pgr.at[2, h], at(i, z, twin))
    for h in range(2):
        side = q // 2 if h == 0 else 1 - q // 2
        remote(prod.at[twin, side], prod.at[twin, side], pgs.at[1, h], pgr.at[1, h], at(i, z, twin)).wait_recv()
        remote(
            prod.at[far_twin, 1 - side], prod.at[far_twin, 1 - side], pgs.at[2, h], pgr.at[2, h], at(i, z, twin)
        ).wait_recv()

    def share(k, h):
        total = jnp.zeros((LANES, HALF), F32)
        for p in range(Q):
            total += jnp.dot(
                restrict[k, :, p * FINE : (p + 1) * FINE], prod[p, h], preferred_element_type=F32
            )
        return total

    half_way = nr // 2
    home = row_of(i)

    def leg(way, t, h, g):
        to = hop(z, 1 if way == 0 else nr - 1)
        row = home if t == half_way - 1 else i
        part = (way, t, h, pl.ds(g * BS, BS))
        return remote(
            outgoing.at[part], incoming.at[part], fs.at[way, t, h, g], fr.at[way, t, h, g], at(row, to, q)
        )

    for t in range(half_way):
        for other in (True, False):
            if t == 0 and other:
                continue
            for way in range(2):
                far_z = hop(z, half_way - t if way == 0 else nr - half_way + t)
                held[way] = share(far_z, 1 - way if other else way)
            for g in range(2):
                for way in range(2):
                    h = 1 - way if other else way
                    rows = pl.ds(g * BS, BS)
                    total = held[way, rows]
                    if t > 1 or (t == 1 and not other):
                        leg(way, t - 1, h, g).wait_recv()
                        total += incoming[way, t - 1, h, rows].astype(F32)
                    outgoing[way, t, h, rows] = total.astype(BF16)
                    launch(leg(way, t, h, g))
        if t == 0:
            for h in range(2):
                own[h] = share(z, h)

            @pl.when(upper)
            def _():
                own_out[...] = own[...].astype(BF16)
                remote(own_out, own_in, os, orc, at(mate, z, q)).start()

    @pl.when(upper)
    def _():
        remote(own_out, own_in, os, orc, at(mate, z, q)).wait()
        own[...] = own_in[...].astype(F32)

    for g in range(2):
        rows = pl.ds(g * BS, BS)
        for h in range(2):
            total = own[h, rows]
            for way in range(2):
                if half_way == 1 and h != way:
                    continue
                leg(way, half_way - 1, h, g).wait_recv()
                total += incoming[way, half_way - 1, h, rows].astype(F32)
            out_ref[rows, h * HALF : (h + 1) * HALF] = total

    for copy in sent:
        copy.wait_send()
    for d in away:
        k_copy(d).wait_send()
        p_copy(d).wait_send()

    @pl.when(jnp.logical_not(here))
    def _():
        k_copy(0).wait_send()
        p_copy(0).wait_send()

    for k in range(nr):
        from_twin(far, 2, k).wait_send()

        @pl.when(k != z)
        def _():
            remote(cbuf.at[k], tbuf.at[z], c2s.at[k], c2r.at[z], at(i, k, q)).wait_send()


def solution(mesh):
    nr = mesh.shape["row"]
    ny = nr // 2

    def shards(a_values, a_rows, a_cols, a_count, p_values, p_rows, p_cols, p_count):
        dma = lambda *n: pltpu.SemaphoreType.DMA(n)
        vmem = pl.BlockSpec(memory_space=pltpu.VMEM)
        return pl.pallas_call(
            functools.partial(kernel, nr),
            out_shape=jax.ShapeDtypeStruct((CB_DEV * BS, 2 * HALF), F32),
            in_specs=[pl.BlockSpec(memory_space=pltpu.HBM)] * 8,
            out_specs=vmem,
            scratch_shapes=[
                pltpu.SMEM((1, SLOTS_A), jnp.int32),
                pltpu.SMEM((1, SLOTS_A), jnp.int32),
                pltpu.SMEM((1, 1), jnp.int32),
                pltpu.SMEM((1, SLOTS_P), jnp.int32),
                pltpu.SMEM((1, SLOTS_P), jnp.int32),
                pltpu.SMEM((1, 1), jnp.int32),
                pltpu.VMEM((1, SLOTS_A, BS * BS), BF16),
                pltpu.VMEM((1, SLOTS_P, BS * BS), BF16),
                pltpu.VMEM((SLOTS_A * BS // 2, LANES), F32),
                pltpu.VMEM((SLOTS_A * BS // 2, LANES), F32),
                pltpu.VMEM((nr, A_ROWS, LANES), BF16),
                pltpu.VMEM((nr, P_ROWS, LANES), BF16),
                pltpu.VMEM((nr, P_ROWS, LANES), BF16),
                pltpu.VMEM((Q, nr, PAIRS_P * BS, LANES), BF16),
                pltpu.VMEM((Q, nr, 1, LANES), F32),
                pltpu.VMEM((1, LANES), F32),
                pltpu.VMEM((nr, FINE, SLOTS_A * BS), BF16),
                pltpu.VMEM((SLOTS_A * BS, HALF), BF16),
                pltpu.VMEM((SLOTS_A * BS, HALF), BF16),
                pltpu.VMEM((nr, LANES, Q * FINE), BF16),
                pltpu.VMEM((FINE, HALF), F32),
                pltpu.VMEM((Q, 2, FINE, HALF), BF16),
                pltpu.VMEM((2, ny, 2, LANES, HALF), BF16),
                pltpu.VMEM((2, ny, 2, LANES, HALF), BF16),
                pltpu.VMEM((2, LANES, HALF), F32),
                pltpu.VMEM((2, LANES, HALF), BF16),
                pltpu.VMEM((2, LANES, HALF), BF16),
                pltpu.VMEM((2, LANES, HALF), F32),
                dma(8), dma(nr), dma(nr), dma(3), dma(3), dma(nr), dma(nr), dma(nr), dma(nr),
                dma(2), dma(2), dma(ny), dma(ny), dma(ny), dma(ny),
                dma(nr), dma(nr),
                dma(3, nr), dma(3, nr),
                dma(3, 2), dma(3, 2),
                dma(2, ny, 2, 2), dma(2, ny, 2, 2),
                pltpu.SemaphoreType.DMA, pltpu.SemaphoreType.DMA,
            ],
            compiler_params=pltpu.CompilerParams(
                collective_id=0, has_side_effects=True, vmem_limit_bytes=40 * 2**20
            ),
        )(
            a_rows, a_cols, a_count, p_rows, p_cols, p_count,
            a_values, p_values,
        )

    return jax.shard_map(
        shards,
        mesh=mesh,
        in_specs=(
            P("col", "row", None),
            P("col", "row"),
            P("col", "row"),
            P("col", "row"),
            P("row", "col", None),
            P("row", "col"),
            P("row", "col"),
            P("row", "col"),
        ),
        out_specs=P("col", "row"),
        check_vma=False,
    )
```
